32 devices in a mesh: ctx: 8 (over y, x, core), section: 4 (over z).
Axes of the slice: x: 2, y: 2, z: 4, core: 2. Of those that a mesh axis runs over, the one named last changes fastest.
Arguments:
- queries: bfloat16 [4, 2048, 2048], P('section', 'ctx'), may hold values from -9 to 9
- keys: bfloat16 [4, 2048, 2048], P('section', 'ctx'), may hold values from -9 to 9
- values: bfloat16 [4, 2048, 2048], P('section', 'ctx'), may hold values from -6 to 6
- segments: int32 [4, 2048], replicated, may hold values from 0 to 1, as said below
- gain_query: bfloat16 [4, 2048], P('section'), may hold values from 0.099609375 to 1.8984375
- gain_key: bfloat16 [4, 2048], P('section'), may hold values from 0.099609375 to 1.8984375
Outputs:
- mixed: bfloat16 [4, 2048, 2048], P('section', 'ctx')
The draws below stay inside these ranges and needn't reach their ends.
Inputs may be any that keep to these rules, and one draw needn't show every extreme that they name: `segments`: along the events of a micro-batch the ids never fall and each of the two ids 0, 1 is used.
All inputs are finite; a program needn't handle non-finite values.
Results may differ from the reference program's by a relative error of at most 0.004.
The reference program's roundings to bfloat16 on the way count: a program that leaves them out, or rounds other values in their place, can miss the bound.
Values may be sent and summed in bfloat16 or wider, within the bound.
A program may use at most 64 MiB of HBM per device.

```python
import math
import jax
import jax.numpy as jnp
from jax import lax

H = 16
HD = 128
TOK_DEV = 256
HOPS = 3
WINDOW = 768
TOKENS = 2048
SECTIONS = 4


def shared_pair(key):
    base = jax.random.fold_in(key, 4242)
    first_key, second_key = jax.random.split(base, 2)
    shape = (SECTIONS, TOKENS, H * HD)
    query_raw = jnp.clip(jax.random.normal(first_key, shape, jnp.float32), -8.0, 8.0)
    key_raw = jnp.clip(jax.random.normal(second_key, shape, jnp.float32), -8.0, 8.0)
    return (query_raw, key_raw)


def draw_queries(key, part):
    return shared_pair(key)[0].astype(jnp.bfloat16)


def draw_keys(key, part):
    return shared_pair(key)[1].astype(jnp.bfloat16)


def draw_segments(key, part):
    base = jax.random.fold_in(key, 7171)
    cut = jax.random.randint(base, (SECTIONS, 1), TOKENS // 4, 3 * TOKENS // 4)
    position = jnp.arange(TOKENS, dtype=jnp.int32)[None, :]
    return (position >= cut).astype(jnp.int32)


def block_levels(own_key, dims, pieces, least, top_value):
    def one(dim, shards_of):
        heights = jax.random.uniform(jax.random.fold_in(jax.random.fold_in(own_key, 6), dim), (shards_of,), jnp.float32, least / len(pieces), top_value / len(pieces))
        return jnp.repeat(jnp.exp(heights), dims[dim] // shards_of).reshape((-1,) + (1,) * (len(dims) - dim - 1))

    factor_of = one(*pieces[0])
    for cut in pieces[1:]:
        factor_of = factor_of * one(*cut)
    return factor_of


def noise(own_key, extent, width, reach, cuts=(), kind=jnp.bfloat16):
    drawn = width * jax.random.normal(own_key, extent, jnp.float32)
    if cuts:
        drawn = drawn * block_levels(own_key, extent, cuts, -0.22, 0.18)
    return jnp.clip(drawn, -reach, reach).astype(kind)


def setup_inputs(seed: int = 0) -> dict:
    streams_of = jax.random.split(jax.random.key(seed), 7)
    return {
        "queries": draw_queries(jax.random.fold_in(streams_of[6], 71), 0),
        "keys": draw_keys(jax.random.fold_in(streams_of[6], 71), 0),
        "values": noise(streams_of[2], (SECTIONS, TOKENS, H * HD), 1.0, 6.0, ((0, 4), (1, 8))),
        "segments": draw_segments(jax.random.fold_in(streams_of[6], 71), 0),
        "gain_query": jnp.clip(1.0 + 0.18 * jax.random.normal(streams_of[4], (SECTIONS, H * HD), jnp.float32), 0.099609375, 1.8984375).astype(jnp.bfloat16),
        "gain_key": jnp.clip(1.0 + 0.18 * jax.random.normal(streams_of[5], (SECTIONS, H * HD), jnp.float32), 0.099609375, 1.8984375).astype(jnp.bfloat16),
    }


NEG = -1e+30

def attend_all(queries, keys, values, segrow, score_scale):
    token_count = queries.shape[0]
    full_width = queries.shape[1]
    head_count = full_width // HD
    span = (HOPS + 1) * TOK_DEV
    block_count = token_count // TOK_DEV
    padded_keys = jnp.concatenate([jnp.zeros((HOPS * TOK_DEV, full_width), keys.dtype), keys], axis=0)
    padded_values = jnp.concatenate([jnp.zeros((HOPS * TOK_DEV, full_width), values.dtype), values], axis=0)
    padded_seg = jnp.concatenate([jnp.full((HOPS * TOK_DEV,), -1, jnp.int32), segrow.astype(jnp.int32)])

    def one_block(block_index):
        start = (block_index * TOK_DEV).astype(jnp.int32)
        query_b = lax.dynamic_slice_in_dim(queries, start, TOK_DEV, 0).astype(jnp.float32).reshape(TOK_DEV, head_count, HD)
        key_b = lax.dynamic_slice_in_dim(padded_keys, start, span, 0).astype(jnp.float32).reshape(span, head_count, HD)
        value_b = lax.dynamic_slice_in_dim(padded_values, start, span, 0).astype(jnp.float32).reshape(span, head_count, HD)
        query_seg = lax.dynamic_slice_in_dim(segrow.astype(jnp.int32), start, TOK_DEV, 0)
        key_seg = lax.dynamic_slice_in_dim(padded_seg, start, span, 0)
        query_pos = start + jnp.arange(TOK_DEV, dtype=jnp.int32)
        key_pos = start - HOPS * TOK_DEV + jnp.arange(span, dtype=jnp.int32)
        allowed = (query_seg[:, None] == key_seg[None, :]) & (key_pos[None, :] <= query_pos[:, None]) & (key_pos[None, :] > query_pos[:, None] - WINDOW) & (key_seg[None, :] >= 0)
        scores = jnp.einsum('qhd,khd->hqk', query_b, key_b) * score_scale
        scores = jnp.where(allowed[None], scores, NEG)
        row_max = lax.optimization_barrier(jnp.max(scores, axis=2, keepdims=True))
        probs = jnp.where(allowed[None], jnp.exp(scores - row_max), 0.0)
        row_total = lax.optimization_barrier(jnp.sum(probs, axis=2))
        rounded = lax.optimization_barrier(probs.astype(jnp.bfloat16)).astype(jnp.float32)
        result = jnp.einsum('hqk,khd->qhd', rounded, value_b) / jnp.transpose(row_total)[:, :, None]
        return result.reshape(TOK_DEV, full_width).astype(jnp.bfloat16)
    blocks = lax.map(one_block, jnp.arange(block_count, dtype=jnp.int32))
    return blocks.reshape(token_count, full_width)

def normalize(received):
    shaped = received.astype(jnp.float32).reshape(received.shape[0], received.shape[1], -1, HD)
    mean_square = lax.optimization_barrier(jnp.mean(shaped * shaped, axis=3, keepdims=True))
    return (shaped * lax.rsqrt(mean_square + 1e-06)).reshape(received.shape).astype(jnp.bfloat16)

def reference(queries, keys, values, segments, gain_query, gain_key):
    first_scale = 1.0 / math.sqrt(HD)
    second_scale = 1.0 / HD

    def first_layer(items):
        return attend_all(items[0], items[1], items[2], items[3], first_scale)

    def second_layer(items):
        return attend_all(items[0], items[1], items[2], items[3], second_scale)
    first_out = lax.map(first_layer, (queries, keys, values, segments))
    received = jnp.roll(first_out, 1, axis=0)
    prior_seg = jnp.roll(segments, 1, axis=0)
    normed = normalize(received)
    normed_f = normed.astype(jnp.float32)
    query_two = (normed_f * gain_query.astype(jnp.float32)[:, None, :]).astype(jnp.bfloat16)
    key_two = (normed_f * gain_key.astype(jnp.float32)[:, None, :]).astype(jnp.bfloat16)
    second = lax.map(second_layer, (query_two, key_two, normed, prior_seg))
    mixed = (second.astype(jnp.float32) + normed_f).astype(jnp.bfloat16)
    return mixed
```

```python
import math

import jax
import jax.numpy as jnp
from jax import lax
from jax.experimental import pallas as pl
from jax.experimental.pallas import tpu as pltpu
from jax.sharding import PartitionSpec as P

HD = 128
HOPS = 3
NEG = -1e30
LOG2E = 1.4426950408889634
MESH = pl.DeviceIdType.MESH


def attend(q, k, v, low, scale):
    rows = q.shape[0]
    span = (HOPS + 1) * rows
    s = lax.dot_general(q, k, (((1,), (1,)), ((), ())), preferred_element_type=jnp.float32)
    row = lax.broadcasted_iota(jnp.int32, (rows, rows), 0)
    col = lax.broadcasted_iota(jnp.int32, (rows, rows), 1)
    new = col <= row
    place = jnp.where(new, col, col - HOPS * rows)
    merged = jnp.where(new, s[:, HOPS * rows :], s[:, :rows])
    parts = [jnp.where(place >= low, merged, NEG)]
    for j in range(1, HOPS):
        parts.append(jnp.where(col + (j - HOPS) * rows >= low, s[:, j * rows : (j + 1) * rows], NEG))
    top = parts[0]
    for part in parts[1:]:
        top = jnp.maximum(top, part)
    m = jnp.max(top, axis=1, keepdims=True)
    probs = [jnp.exp2((part - m) * (scale * LOG2E)) for part in parts]
    total = probs[0]
    for prob in probs[1:]:
        total = total + prob
    l = jnp.sum(total, axis=1, keepdims=True)
    old_p = jnp.where(new, 0.0, probs[0]).astype(jnp.bfloat16)
    new_p = jnp.where(new, probs[0], 0.0).astype(jnp.bfloat16)
    pb = jnp.concatenate([old_p] + [x.astype(jnp.bfloat16) for x in probs[1:]] + [new_p], axis=1)
    out = jnp.dot(pb, v, preferred_element_type=jnp.float32)
    return (out / l).astype(jnp.bfloat16)


def make_kernel(ctx, sections, group, rows, heads_here):
    groups = ctx // group
    pad = HOPS * rows
    width = heads_here * HD

    def kernel(q_in, k_in, v_in, seg, gq, gk, out, qb, kb, vb, fb, xb, nb, k2b, ob,
               in_send, in_recv, z_send, z_recv, o_send, o_recv, *halo):
        c = lax.axis_index("ctx")
        s = lax.axis_index("section")
        grp = c // group
        me = c % group
        base = grp * group
        ahead = lax.rem(s + 1, sections)
        behind = lax.rem(s + sections - 1, sections)
        next_base = lax.rem(grp + 1, groups) * group
        prev_base = lax.rem(grp + groups - 1, groups) * group

        def rows_of(b, count=1):
            return pl.ds(pl.multiple_of(b * rows, rows), count * rows)

        def peer(k):
            return base + lax.rem(me + k, group)

        def cols_of(p, h):
            return pl.ds(pl.multiple_of(lax.rem(p, group) * width + h * HD, HD), HD)

        barrier = pltpu.get_barrier_semaphore()

        def greet(k, carry):
            pl.semaphore_signal(barrier, inc=1, device_id=(peer(k), s), device_id_type=MESH)
            return carry

        lax.fori_loop(1, group, greet, 0)
        pl.semaphore_signal(barrier, inc=1, device_id=(c, ahead), device_id_type=MESH)
        pl.semaphore_signal(barrier, inc=1, device_id=(c, behind), device_id_type=MESH)
        expected = group + 1
        if groups > 1:
            def greet_far(k, carry):
                pl.semaphore_signal(barrier, inc=1, device_id=(next_base + k, s), device_id_type=MESH)
                pl.semaphore_signal(barrier, inc=1, device_id=(prev_base + k, s), device_id_type=MESH)
                return carry

            lax.fori_loop(0, group, greet_far, 0)
            pl.semaphore_signal(barrier, inc=1, device_id=(next_base + me, ahead), device_id_type=MESH)
            pl.semaphore_signal(barrier, inc=1, device_id=(prev_base + me, behind), device_id_type=MESH)
            expected = expected + 2 * group + 2

        ins = (q_in, k_in, v_in)
        bufs = (qb, kb, vb)
        lead = (0, HOPS, HOPS)

        def own_copy(a, h):
            return pltpu.make_async_copy(
                ins[a].at[0, :, cols_of(me, h)], bufs[a].at[h, rows_of(me + lead[a])], in_recv.at[a, h, 0]
            )

        def in_copy(a, h, k, place):
            p = peer(k)
            return pltpu.make_async_remote_copy(
                src_ref=ins[a].at[0, :, cols_of(p, h)],
                dst_ref=bufs[a].at[h, rows_of(place + lead[a])],
                send_sem=in_send.at[a, h, k],
                recv_sem=in_recv.at[a, h, k],
                device_id=(p, s),
                device_id_type=MESH,
            )

        for h in range(heads_here):
            for a in range(3):
                own_copy(a, h).start()
        if groups == 1:
            zero = jnp.zeros((heads_here, pad, HD), jnp.bfloat16)
            kb[:, :pad, :] = zero
            vb[:, :pad, :] = zero
            k2b[:, :pad, :] = zero
            nb[:, :pad, :] = zero
        pl.semaphore_wait(barrier, expected)

        def send_in(t, carry):
            h = t // (group - 1)
            k = 1 + lax.rem(t, group - 1)
            for a in range(3):
                in_copy(a, h, k, me).start()
            return carry

        lax.fori_loop(0, heads_here * (group - 1), send_in, 0)

        if groups > 1:
            hi_send, hi_recv, hz_send, hz_recv = halo

            def halo_in(a, h, k, j):
                return pltpu.make_async_remote_copy(
                    src_ref=ins[a].at[0, :, cols_of(k, h)],
                    dst_ref=bufs[a].at[h, rows_of(j)],
                    send_sem=hi_send.at[a - 1, h, k],
                    recv_sem=hi_recv.at[a - 1, h, j],
                    device_id=(next_base + k, s),
                    device_id_type=MESH,
                )

            def halo_z(h, j, b):
                return pltpu.make_async_remote_copy(
                    src_ref=fb.at[h, rows_of(b)],
                    dst_ref=nb.at[h, rows_of(j)],
                    send_sem=hz_send.at[h, j],
                    recv_sem=hz_recv.at[h, j],
                    device_id=(next_base + me, ahead),
                    device_id_type=MESH,
                )

            @pl.when(me >= group - HOPS)
            def _():
                def send_halo(t, carry):
                    for a in (1, 2):
                        halo_in(a, t // group, lax.rem(t, group), me - (group - HOPS)).start()
                    return carry

                lax.fori_loop(0, heads_here * group, send_halo, 0)

        pos = lax.broadcasted_iota(jnp.int32, (rows, 1), 0)

        def zeros_in(which):
            ids = seg[pl.ds(which, 1), :]
            return jnp.sum(jnp.where(ids == 0, 1.0, 0.0), axis=1, keepdims=True).astype(jnp.int32)

        def low_of(b, cut):
            first = (base + b) * rows
            return jnp.where(pos + first >= cut, cut, 0) - first

        def z_copy(h, b, slot):
            return pltpu.make_async_remote_copy(
                src_ref=fb.at[h, rows_of(b)],
                dst_ref=xb.at[h, rows_of(b)],
                send_sem=z_send.at[h, slot],
                recv_sem=z_recv.at[h, slot],
                device_id=(c, ahead),
                device_id_type=MESH,
            )

        own_cut = zeros_in(s)
        start = lax.rem(me + group - HOPS, group)

        def layer_one(t, carry):
            h = t // group
            i = lax.rem(t, group)

            @pl.when(i == 0)
            def _():
                for a in range(3):
                    own_copy(a, h).wait()

                def arrived(k, inner):
                    for a in range(3):
                        in_copy(a, h, k, lax.rem(me + group - k, group)).wait_recv()
                    return inner

                lax.fori_loop(1, group, arrived, 0)
                if groups > 1:
                    for a in (1, 2):
                        for j in range(HOPS):
                            halo_in(a, h, j, j).wait_recv()

            b = lax.rem(start + i, group)
            fb[h, rows_of(b)] = attend(
                qb[h, rows_of(b)],
                kb[h, rows_of(b, HOPS + 1)],
                vb[h, rows_of(b, HOPS + 1)],
                low_of(b, own_cut),
                1.0 / math.sqrt(HD),
            )
            z_copy(h, b, i).start()
            if groups > 1:
                @pl.when(b >= group - HOPS)
                def _():
                    halo_z(h, b - (group - HOPS), b).start()
            return carry

        lax.fori_loop(0, heads_here * group, layer_one, 0)

        prior_cut = zeros_in(behind)

        def normalize(x):
            x = x.astype(jnp.float32)
            mean = jnp.mean(x * x, axis=1, keepdims=True)
            return (x * lax.rsqrt(mean + 1e-06)).astype(jnp.bfloat16)

        def gained(normed, gain, h):
            g = gain[:, cols_of(me, h)].astype(jnp.float32)
            return (normed.astype(jnp.float32) * g).astype(jnp.bfloat16)

        def take(h, slot):
            b = lax.rem(start + slot, group)
            z_copy(h, b, slot).wait_recv()
            normed = normalize(xb[h, rows_of(b)])
            nb[h, rows_of(b + HOPS)] = normed
            k2b[h, rows_of(b + HOPS)] = gained(normed, gk, h)

        def out_copy(h, k):
            return pltpu.make_async_remote_copy(
                src_ref=ob.at[h, rows_of(lax.rem(me + k, group))],
                dst_ref=out.at[0, :, cols_of(me, h)],
                send_sem=o_send.at[h, k],
                recv_sem=o_recv.at[h, k],
                device_id=(peer(k), s),
                device_id_type=MESH,
            )

        def out_own(h):
            return pltpu.make_async_copy(
                ob.at[h, rows_of(me)], out.at[0, :, cols_of(me, h)], o_recv.at[h, 0]
            )

        def layer_two(t, carry):
            h = t // group
            i = lax.rem(t, group)

            @pl.when(i == 0)
            def _():
                if groups > 1:
                    for j in range(HOPS):
                        halo_z(h, j, j).wait_recv()
                        normed = normalize(nb[h, rows_of(j)])
                        nb[h, rows_of(j)] = normed
                        k2b[h, rows_of(j)] = gained(normed, gk, h)

                def first_ones(slot, inner):
                    take(h, slot)
                    return inner

                lax.fori_loop(0, HOPS, first_ones, 0)

            @pl.when(i < group - HOPS)
            def _():
                take(h, i + HOPS)

            b = lax.rem(me + i, group)
            normed = nb[h, rows_of(b + HOPS)]
            second = attend(
                gained(normed, gq, h),
                k2b[h, rows_of(b, HOPS + 1)],
                nb[h, rows_of(b, HOPS + 1)],
                low_of(b, prior_cut),
                1.0 / HD,
            )
            ob[h, rows_of(b)] = (second.astype(jnp.float32) + normed.astype(jnp.float32)).astype(jnp.bfloat16)

            @pl.when(i == 0)
            def _():
                out_own(h).start()

            @pl.when(i > 0)
            def _():
                out_copy(h, i).start()

            return carry

        lax.fori_loop(0, heads_here * group, layer_two, 0)

        def finish(t, carry):
            h = t // (group - 1)
            k = 1 + lax.rem(t, group - 1)
            for a in range(3):
                in_copy(a, h, k, me).wait_send()
            out_copy(h, k).wait_send()
            p = lax.rem(me + group - k, group)
            pltpu.make_async_remote_copy(
                src_ref=ob.at[h, rows_of(me)],
                dst_ref=out.at[0, :, cols_of(p, h)],
                send_sem=o_send.at[h, k],
                recv_sem=o_recv.at[h, k],
                device_id=(peer(k), s),
                device_id_type=MESH,
            ).wait_recv()
            return carry

        lax.fori_loop(0, heads_here * (group - 1), finish, 0)

        def finish_z(t, carry):
            h = t // group
            i = lax.rem(t, group)
            z_copy(h, lax.rem(start + i, group), i).wait_send()
            return carry

        lax.fori_loop(0, heads_here * group, finish_z, 0)
        for h in range(heads_here):
            out_own(h).wait()
            if groups > 1:
                for j in range(HOPS):
                    halo_z(h, j, group - HOPS + j).wait_send()
        if groups > 1:
            @pl.when(me >= group - HOPS)
            def _():
                def sent_halo(t, carry):
                    for a in (1, 2):
                        halo_in(a, t // group, lax.rem(t, group), me - (group - HOPS)).wait_send()
                    return carry

                lax.fori_loop(0, heads_here * group, sent_halo, 0)

    return kernel


def solution(mesh):
    ctx = mesh.shape["ctx"]
    sections = mesh.shape["section"]
    group = math.gcd(ctx, 8)

    def per_device(queries, keys, values, segments, gain_query, gain_key):
        _, rows, width = queries.shape
        heads_here = width // HD // group
        padded = (group + HOPS) * rows
        bf = jnp.bfloat16
        dma = pltpu.SemaphoreType.DMA
        scratch = [
            pltpu.VMEM((heads_here, group * rows, HD), bf),
            pltpu.VMEM((heads_here, padded, HD), bf),
            pltpu.VMEM((heads_here, padded, HD), bf),
            pltpu.VMEM((heads_here, group * rows, HD), bf),
            pltpu.VMEM((heads_here, group * rows, HD), bf),
            pltpu.VMEM((heads_here, padded, HD), bf),
            pltpu.VMEM((heads_here, padded, HD), bf),
            pltpu.VMEM((heads_here, group * rows, HD), bf),
            dma((3, heads_here, group)),
            dma((3, heads_here, group)),
            dma((heads_here, group)),
            dma((heads_here, group)),
            dma((heads_here, group)),
            dma((heads_here, group)),
        ]
        if ctx > group:
            scratch += [
                dma((2, heads_here, group)),
                dma((2, heads_here, HOPS)),
                dma((heads_here, HOPS)),
                dma((heads_here, HOPS)),
            ]
        hbm = pl.BlockSpec(memory_space=pl.ANY)
        vmem = pl.BlockSpec(memory_space=pltpu.VMEM)
        return pl.pallas_call(
            make_kernel(ctx, sections, group, rows, heads_here),
            out_shape=jax.ShapeDtypeStruct(queries.shape, bf),
            in_specs=[hbm, hbm, hbm, vmem, vmem, vmem],
            out_specs=hbm,
            scratch_shapes=scratch,
            compiler_params=pltpu.CompilerParams(
                collective_id=0, has_side_effects=True, vmem_limit_bytes=48 * 1024 * 1024
            ),
        )(queries, keys, values, segments, gain_query, gain_key)

    return jax.shard_map(
        per_device,
        mesh=mesh,
        in_specs=(
            P("section", "ctx", None),
            P("section", "ctx", None),
            P("section", "ctx", None),
            P(),
            P("section", None),
            P("section", None),
        ),
        out_specs=P("section", "ctx", None),
        check_vma=False,
    )
```

```python
import math

import jax
import jax.numpy as jnp
from jax import lax
from jax.experimental import pallas as pl
from jax.experimental.pallas import tpu as pltpu
from jax.sharding import PartitionSpec as P

HD = 128
HOPS = 3
NEG = -1e30
LOG2E = 1.4426950408889634
MESH = pl.DeviceIdType.MESH


def score_of(q, k):
    return lax.dot_general(q, k, (((1,), (1,)), ((), ())), preferred_element_type=jnp.float32)


def weights_of(s, low, scale, shift):
    rows = s.shape[0]
    row = lax.broadcasted_iota(jnp.int32, (rows, rows), 0)
    col = lax.broadcasted_iota(jnp.int32, (rows, rows), 1)
    new = col <= row
    place = jnp.where(new, col, col - HOPS * rows)
    merged = jnp.where(new, s[:, HOPS * rows :], s[:, :rows])
    parts = [jnp.where(place >= low, merged, NEG)]
    for j in range(1, HOPS):
        parts.append(jnp.where(col + (j - HOPS) * rows >= low, s[:, j * rows : (j + 1) * rows], NEG))
    if shift:
        top = parts[0]
        for part in parts[1:]:
            top = jnp.maximum(top, part)
        m = jnp.max(top, axis=1, keepdims=True)
        parts = [part - m for part in parts]
    probs = [jnp.exp2(part * (scale * LOG2E)) for part in parts]
    total = probs[0]
    for prob in probs[1:]:
        total = total + prob
    l = jnp.sum(total, axis=1, keepdims=True)
    old_p = jnp.where(new, 0.0, probs[0]).astype(jnp.bfloat16)
    new_p = jnp.where(new, probs[0], 0.0).astype(jnp.bfloat16)
    return jnp.concatenate([old_p] + [x.astype(jnp.bfloat16) for x in probs[1:]] + [new_p], axis=1), l


def attend_all(tiles, scale, shift):
    scores = [score_of(q, k) for q, k, _, _ in tiles]
    outs = []
    for s, (_, _, v, low) in zip(scores, tiles):
        pb, l = weights_of(s, low, scale, shift)
        out = jnp.dot(pb, v, preferred_element_type=jnp.float32)
        outs.append((out / l).astype(jnp.bfloat16))
    return outs


def make_kernel(ctx, sections, group, rows, heads_here):
    groups = ctx // group
    pad = HOPS * rows
    width = heads_here * HD

    def kernel(q_in, k_in, v_in, seg_in, gq_in, gk_in, out, qb, kb, vb, fb, xb, nb, k2b, ob, seg, gq, gk,
               small, in_send, in_recv, z_send, z_recv, o_send, o_recv, *halo):
        c = lax.axis_index("ctx")
        s = lax.axis_index("section")
        grp = c // group
        me = c % group
        base = grp * group
        ahead = lax.rem(s + 1, sections)
        behind = lax.rem(s + sections - 1, sections)
        next_base = lax.rem(grp + 1, groups) * group
        prev_base = lax.rem(grp + groups - 1, groups) * group

        def rows_of(b, count=1):
            return pl.ds(pl.multiple_of(b * rows, rows), count * rows)

        def peer(k):
            return base + lax.rem(me + k, group)

        def cols_of(p, h):
            return pl.ds(pl.multiple_of(lax.rem(p, group) * width + h * HD, HD), HD)

        barrier = pltpu.get_barrier_semaphore()

        def greet(k, carry):
            pl.semaphore_signal(barrier, inc=1, device_id=(peer(k), s), device_id_type=MESH)
            return carry

        lax.fori_loop(1, group, greet, 0)
        pl.semaphore_signal(barrier, inc=1, device_id=(c, ahead), device_id_type=MESH)
        pl.semaphore_signal(barrier, inc=1, device_id=(c, behind), device_id_type=MESH)
        expected = group + 1
        if groups > 1:
            def greet_far(k, carry):
                pl.semaphore_signal(barrier, inc=1, device_id=(next_base + k, s), device_id_type=MESH)
                pl.semaphore_signal(barrier, inc=1, device_id=(prev_base + k, s), device_id_type=MESH)
                return carry

            lax.fori_loop(0, group, greet_far, 0)
            pl.semaphore_signal(barrier, inc=1, device_id=(next_base + me, ahead), device_id_type=MESH)
            pl.semaphore_signal(barrier, inc=1, device_id=(prev_base + me, behind), device_id_type=MESH)
            expected = expected + 2 * group + 2

        ins = (q_in, k_in, v_in)
        bufs = (qb, kb, vb)
        lead = (0, HOPS, HOPS)

        def own_copy(a, h):
            return pltpu.make_async_copy(
                ins[a].at[0, :, cols_of(me, h)], bufs[a].at[h, rows_of(me + lead[a])], in_recv.at[a, h, 0]
            )

        def in_copy(a, h, k, place):
            p = peer(k)
            return pltpu.make_async_remote_copy(
                src_ref=ins[a].at[0, :, cols_of(p, h)],
                dst_ref=bufs[a].at[h, rows_of(place + lead[a])],
                send_sem=in_send.at[a, h, k],
                recv_sem=in_recv.at[a, h, k],
                device_id=(p, s),
                device_id_type=MESH,
            )

        smalls = [
            pltpu.make_async_copy(src, dst, small.at[j])
            for j, (src, dst) in enumerate(((seg_in, seg), (gq_in, gq), (gk_in, gk)))
        ]
        for copy in smalls:
            copy.start()
        for h in range(heads_here):
            for a in range(3):
                own_copy(a, h).start()
        if groups == 1:
            zero = jnp.zeros((heads_here, pad, HD), jnp.bfloat16)
            kb[:, :pad, :] = zero
            vb[:, :pad, :] = zero
            k2b[:, :pad, :] = zero
            nb[:, :pad, :] = zero
        pl.semaphore_wait(barrier, expected)

        def send_in(t, carry):
            h = t // (group - 1)
            k = 1 + lax.rem(t, group - 1)

            @pl.when(h > 0)
            def _():
                for a in range(3):
                    in_copy(a, h - 1, k, me).wait_send()

            for a in range(3):
                in_copy(a, h, k, me).start()
            return carry

        lax.fori_loop(0, heads_here * (group - 1), send_in, 0)
        for copy in smalls:
            copy.wait()

        if groups > 1:
            hi_send, hi_recv, hz_send, hz_recv = halo

            def halo_in(a, h, k, j):
                return pltpu.make_async_remote_copy(
                    src_ref=ins[a].at[0, :, cols_of(k, h)],
                    dst_ref=bufs[a].at[h, rows_of(j)],
                    send_sem=hi_send.at[a - 1, h, k],
                    recv_sem=hi_recv.at[a - 1, h, j],
                    device_id=(next_base + k, s),
                    device_id_type=MESH,
                )

            def halo_z(h, j, b):
                return pltpu.make_async_remote_copy(
                    src_ref=fb.at[h, rows_of(b)],
                    dst_ref=nb.at[h, rows_of(j)],
                    send_sem=hz_send.at[h, j],
                    recv_sem=hz_recv.at[h, j],
                    device_id=(next_base + me, ahead),
                    device_id_type=MESH,
                )

            @pl.when(me >= group - HOPS)
            def _():
                def send_halo(t, carry):
                    for a in (1, 2):
                        halo_in(a, t // group, lax.rem(t, group), me - (group - HOPS)).start()
                    return carry

                lax.fori_loop(0, heads_here * group, send_halo, 0)

        pos = lax.broadcasted_iota(jnp.int32, (rows, 1), 0)

        def zeros_in(which):
            ids = seg[pl.ds(which, 1), :]
            return jnp.sum(jnp.where(ids == 0, 1.0, 0.0), axis=1, keepdims=True).astype(jnp.int32)

        def low_of(b, cut):
            first = (base + b) * rows
            return jnp.where(pos + first >= cut, cut, 0) - first

        def z_copy(h, b, slot):
            return pltpu.make_async_remote_copy(
                src_ref=fb.at[h, rows_of(b)],
                dst_ref=xb.at[h, rows_of(b)],
                send_sem=z_send.at[h, slot],
                recv_sem=z_recv.at[h, slot],
                device_id=(c, ahead),
                device_id_type=MESH,
            )

        own_cut = zeros_in(s)
        start = lax.rem(me + group - HOPS, group)

        def layer_one(t, carry):
            h = t // (group // 2)
            i = 2 * lax.rem(t, group // 2)

            @pl.when(i == 0)
            def _():
                for a in range(3):
                    own_copy(a, h).wait()

                def arrived(k, inner):
                    for a in range(3):
                        in_copy(a, h, k, lax.rem(me + group - k, group)).wait_recv()
                    return inner

                lax.fori_loop(1, group, arrived, 0)
                if groups > 1:
                    for a in (1, 2):
                        for j in range(HOPS):
                            halo_in(a, h, j, j).wait_recv()

            tiles = [lax.rem(start + i + j, group) for j in range(2)]
            results = attend_all(
                [
                    (
                        qb[h, rows_of(b)],
                        kb[h, rows_of(b, HOPS + 1)],
                        vb[h, rows_of(b, HOPS + 1)],
                        low_of(b, own_cut),
                    )
                    for b in tiles
                ],
                1.0 / math.sqrt(HD),
                True,
            )
            for j, (b, result) in enumerate(zip(tiles, results)):
                fb[h, rows_of(b)] = result
                z_copy(h, b, i + j).start()
                if groups > 1:
                    @pl.when(b >= group - HOPS)
                    def _():
                        halo_z(h, b - (group - HOPS), b).start()
            return carry

        lax.fori_loop(0, heads_here * (group // 2), layer_one, 0)

        prior_cut = zeros_in(behind)

        def normalize(x):
            x = x.astype(jnp.float32)
            mean = jnp.mean(x * x, axis=1, keepdims=True)
            return (x * lax.rsqrt(mean + 1e-06)).astype(jnp.bfloat16)

        def gained(normed, gain, h):
            g = gain[:, cols_of(me, h)].astype(jnp.float32)
            return (normed.astype(jnp.float32) * g).astype(jnp.bfloat16)

        def take(h, slot):
            b = lax.rem(start + slot, group)
            z_copy(h, b, slot).wait_recv()
            normed = normalize(xb[h, rows_of(b)])
            nb[h, rows_of(b + HOPS)] = normed
            k2b[h, rows_of(b + HOPS)] = gained(normed, gk, h)

        def out_copy(h, k):
            return pltpu.make_async_remote_copy(
                src_ref=ob.at[h, rows_of(lax.rem(me + k, group))],
                dst_ref=out.at[0, :, cols_of(me, h)],
                send_sem=o_send.at[h, k],
                recv_sem=o_recv.at[h, k],
                device_id=(peer(k), s),
                device_id_type=MESH,
            )

        def out_own(h):
            return pltpu.make_async_copy(
                ob.at[h, rows_of(me)], out.at[0, :, cols_of(me, h)], o_recv.at[h, 0]
            )

        def layer_two(t, carry):
            h = t // (group // 2)
            i = 2 * lax.rem(t, group // 2)

            @pl.when(i == 0)
            def _():
                if groups > 1:
                    for j in range(HOPS):
                        halo_z(h, j, j).wait_recv()
                        normed = normalize(nb[h, rows_of(j)])
                        nb[h, rows_of(j)] = normed
                        k2b[h, rows_of(j)] = gained(normed, gk, h)

                def first_ones(slot, inner):
                    take(h, slot)
                    return inner

                lax.fori_loop(0, HOPS, first_ones, 0)

            for j in range(2):
                @pl.when(i + j < group - HOPS)
                def _():
                    take(h, i + j + HOPS)

            tiles = [lax.rem(me + i + j, group) for j in range(2)]
            normed = [nb[h, rows_of(b + HOPS)] for b in tiles]
            results = attend_all(
                [
                    (
                        gained(own, gq, h),
                        k2b[h, rows_of(b, HOPS + 1)],
                        nb[h, rows_of(b, HOPS + 1)],
                        low_of(b, prior_cut),
                    )
                    for b, own in zip(tiles, normed)
                ],
                1.0 / HD,
                False,
            )
            for b, own, second in zip(tiles, normed, results):
                mixed = second.astype(jnp.float32) + own.astype(jnp.float32)
                ob[h, rows_of(b)] = mixed.astype(jnp.bfloat16)

            @pl.when(i == 0)
            def _():
                out_own(h).start()

            @pl.when(i > 0)
            def _():
                out_copy(h, i).start()

            out_copy(h, i + 1).start()
            return carry

        lax.fori_loop(0, heads_here * (group // 2), layer_two, 0)

        def finish(t, carry):
            h = t // (group - 1)
            k = 1 + lax.rem(t, group - 1)
            @pl.when(h == heads_here - 1)
            def _():
                for a in range(3):
                    in_copy(a, h, k, me).wait_send()

            out_copy(h, k).wait_send()
            p = lax.rem(me + group - k, group)
            pltpu.make_async_remote_copy(
                src_ref=ob.at[h, rows_of(me)],
                dst_ref=out.at[0, :, cols_of(p, h)],
                send_sem=o_send.at[h, k],
                recv_sem=o_recv.at[h, k],
                device_id=(peer(k), s),
                device_id_type=MESH,
            ).wait_recv()
            return carry

        lax.fori_loop(0, heads_here * (group - 1), finish, 0)

        def finish_z(t, carry):
            h = t // group
            i = lax.rem(t, group)
            z_copy(h, lax.rem(start + i, group), i).wait_send()
            return carry

        lax.fori_loop(0, heads_here * group, finish_z, 0)
        for h in range(heads_here):
            out_own(h).wait()
            if groups > 1:
                for j in range(HOPS):
                    halo_z(h, j, group - HOPS + j).wait_send()
        if groups > 1:
            @pl.when(me >= group - HOPS)
            def _():
                def sent_halo(t, carry):
                    for a in (1, 2):
                        halo_in(a, t // group, lax.rem(t, group), me - (group - HOPS)).wait_send()
                    return carry

                lax.fori_loop(0, heads_here * group, sent_halo, 0)

    return kernel


def solution(mesh):
    ctx = mesh.shape["ctx"]
    sections = mesh.shape["section"]
    group = math.gcd(ctx, 8)

    def per_device(queries, keys, values, segments, gain_query, gain_key):
        _, rows, width = queries.shape
        heads_here = width // HD // group
        padded = (group + HOPS) * rows
        bf = jnp.bfloat16
        dma = pltpu.SemaphoreType.DMA
        scratch = [
            pltpu.VMEM((heads_here, group * rows, HD), bf),
            pltpu.VMEM((heads_here, padded, HD), bf),
            pltpu.VMEM((heads_here, padded, HD), bf),
            pltpu.VMEM((heads_here, group * rows, HD), bf),
            pltpu.VMEM((heads_here, group * rows, HD), bf),
            pltpu.VMEM((heads_here, padded, HD), bf),
            pltpu.VMEM((heads_here, padded, HD), bf),
            pltpu.VMEM((heads_here, group * rows, HD), bf),
            pltpu.VMEM(segments.shape, segments.dtype),
            pltpu.VMEM(gain_query.shape, bf),
            pltpu.VMEM(gain_key.shape, bf),
            dma((3,)),
            dma((3, heads_here, group)),
            dma((3, heads_here, group)),
            dma((heads_here, group)),
            dma((heads_here, group)),
            dma((heads_here, group)),
            dma((heads_here, group)),
        ]
        if ctx > group:
            scratch += [
                dma((2, heads_here, group)),
                dma((2, heads_here, HOPS)),
                dma((heads_here, HOPS)),
                dma((heads_here, HOPS)),
            ]
        hbm = pl.BlockSpec(memory_space=pl.ANY)
        return pl.pallas_call(
            make_kernel(ctx, sections, group, rows, heads_here),
            out_shape=jax.ShapeDtypeStruct(queries.shape, bf),
            in_specs=[hbm] * 6,
            out_specs=hbm,
            scratch_shapes=scratch,
            compiler_params=pltpu.CompilerParams(
                collective_id=0, has_side_effects=True, vmem_limit_bytes=60 * 1024 * 1024
            ),
        )(queries, keys, values, segments, gain_query, gain_key)

    return jax.shard_map(
        per_device,
        mesh=mesh,
        in_specs=(
            P("section", "ctx", None),
            P("section", "ctx", None),
            P("section", "ctx", None),
            P(),
            P("section", None),
            P("section", None),
        ),
        out_specs=P("section", "ctx", None),
        check_vma=False,
    )
```

```python
import math

import jax
import jax.numpy as jnp
from jax import lax
from jax.experimental import pallas as pl
from jax.experimental.pallas import tpu as pltpu
from jax.sharding import PartitionSpec as P

HD = 128
HOPS = 3
NEG = -1e30
LOG2E = 1.4426950408889634
MESH = pl.DeviceIdType.MESH


def score_of(q, k):
    return lax.dot_general(q, k, (((1,), (1,)), ((), ())), preferred_element_type=jnp.float32)


def weights_of(s, low, scale, shift):
    rows = s.shape[0]
    row = lax.broadcasted_iota(jnp.int32, (rows, rows), 0)
    col = lax.broadcasted_iota(jnp.int32, (rows, rows), 1)
    new = col <= row
    place = jnp.where(new, col, col - HOPS * rows)
    merged = jnp.where(new, s[:, HOPS * rows :], s[:, :rows])
    parts = [jnp.where(place >= low, merged, NEG)]
    for j in range(1, HOPS):
        parts.append(jnp.where(col + (j - HOPS) * rows >= low, s[:, j * rows : (j + 1) * rows], NEG))
    if shift:
        top = parts[0]
        for part in parts[1:]:
            top = jnp.maximum(top, part)
        m = jnp.max(top, axis=1, keepdims=True)
        parts = [part - m for part in parts]
    probs = [jnp.exp2(part * (scale * LOG2E)) for part in parts]
    total = probs[0]
    for prob in probs[1:]:
        total = total + prob
    l = jnp.sum(total, axis=1, keepdims=True)
    old_p = jnp.where(new, 0.0, probs[0]).astype(jnp.bfloat16)
    new_p = jnp.where(new, probs[0], 0.0).astype(jnp.bfloat16)
    return jnp.concatenate([old_p] + [x.astype(jnp.bfloat16) for x in probs[1:]] + [new_p], axis=1), l


def attend_all(tiles, scale, shift):
    scores = [score_of(q, k) for q, k, _, _ in tiles]
    outs = []
    for s, (_, _, v, low) in zip(scores, tiles):
        pb, l = weights_of(s, low, scale, shift)
        out = jnp.dot(pb, v, preferred_element_type=jnp.float32)
        outs.append((out / l).astype(jnp.bfloat16))
    return outs


def make_kernel(ctx, sections, group, rows, heads_here):
    groups = ctx // group
    pad = HOPS * rows
    width = heads_here * HD

    def kernel(q_in, k_in, v_in, seg_in, gq_in, gk_in, out, qb, kb, vb, fb, xb, nb, k2b, ob, seg, gq, gk,
               small, in_send, in_recv, z_send, z_recv, o_send, o_recv, *halo):
        c = lax.axis_index("ctx")
        s = lax.axis_index("section")
        grp = c // group
        me = c % group
        base = grp * group
        ahead = lax.rem(s + 1, sections)
        behind = lax.rem(s + sections - 1, sections)
        next_base = lax.rem(grp + 1, groups) * group
        prev_base = lax.rem(grp + groups - 1, groups) * group

        def rows_of(b, count=1):
            return pl.ds(pl.multiple_of(b * rows, rows), count * rows)

        def peer(k):
            return base + lax.rem(me + k, group)

        def cols_of(p, h):
            return pl.ds(pl.multiple_of(lax.rem(p, group) * width + h * HD, HD), HD)

        barrier = pltpu.get_barrier_semaphore()

        def greet(k, carry):
            pl.semaphore_signal(barrier, inc=1, device_id=(peer(k), s), device_id_type=MESH)
            return carry

        lax.fori_loop(1, group, greet, 0)
        pl.semaphore_signal(barrier, inc=1, device_id=(c, ahead), device_id_type=MESH)
        pl.semaphore_signal(barrier, inc=1, device_id=(c, behind), device_id_type=MESH)
        expected = group + 1
        if groups > 1:
            def greet_far(k, carry):
                pl.semaphore_signal(barrier, inc=1, device_id=(next_base + k, s), device_id_type=MESH)
                pl.semaphore_signal(barrier, inc=1, device_id=(prev_base + k, s), device_id_type=MESH)
                return carry

            lax.fori_loop(0, group, greet_far, 0)
            pl.semaphore_signal(barrier, inc=1, device_id=(next_base + me, ahead), device_id_type=MESH)
            pl.semaphore_signal(barrier, inc=1, device_id=(prev_base + me, behind), device_id_type=MESH)
            expected = expected + 2 * group + 2

        ins = (q_in, k_in, v_in)
        bufs = (qb, kb, vb)
        lead = (0, HOPS, HOPS)

        def own_copy(a, h):
            return pltpu.make_async_copy(
                ins[a].at[0, :, cols_of(me, h)], bufs[a].at[h, rows_of(me + lead[a])], in_recv.at[a, h, 0]
            )

        def in_copy(a, h, k, place):
            p = peer(k)
            return pltpu.make_async_remote_copy(
                src_ref=ins[a].at[0, :, cols_of(p, h)],
                dst_ref=bufs[a].at[h, rows_of(place + lead[a])],
                send_sem=in_send.at[a, h, k],
                recv_sem=in_recv.at[a, h, k],
                device_id=(p, s),
                device_id_type=MESH,
            )

        smalls = [
            pltpu.make_async_copy(src, dst, small.at[j])
            for j, (src, dst) in enumerate(((seg_in, seg), (gq_in, gq), (gk_in, gk)))
        ]
        for copy in smalls:
            copy.start()
        for h in range(heads_here):
            for a in range(3):
                own_copy(a, h).start()
        if groups == 1:
            zero = jnp.zeros((heads_here, pad, HD), jnp.bfloat16)
            kb[:, :pad, :] = zero
            vb[:, :pad, :] = zero
            k2b[:, :pad, :] = zero
            nb[:, :pad, :] = zero
        pl.semaphore_wait(barrier, expected)

        half = group // 2

        def send_in(t, carry):
            h = t // group
            k = lax.rem(t // half + me, 2) + 2 * lax.rem(t, half)

            @pl.when(k > 0)
            def _():
                @pl.when(h > 0)
                def _():
                    for a in range(3):
                        in_copy(a, h - 1, k, me).wait_send()

                for a in range(3):
                    in_copy(a, h, k, me).start()

            return carry

        lax.fori_loop(0, heads_here * group, send_in, 0)
        for copy in smalls:
            copy.wait()

        if groups > 1:
            hi_send, hi_recv, hz_send, hz_recv = halo

            def halo_in(a, h, k, j):
                return pltpu.make_async_remote_copy(
                    src_ref=ins[a].at[0, :, cols_of(k, h)],
                    dst_ref=bufs[a].at[h, rows_of(j)],
                    send_sem=hi_send.at[a - 1, h, k],
                    recv_sem=hi_recv.at[a - 1, h, j],
                    device_id=(next_base + k, s),
                    device_id_type=MESH,
                )

            def halo_z(h, j, b):
                return pltpu.make_async_remote_copy(
                    src_ref=fb.at[h, rows_of(b)],
                    dst_ref=nb.at[h, rows_of(j)],
                    send_sem=hz_send.at[h, j],
                    recv_sem=hz_recv.at[h, j],
                    device_id=(next_base + me, ahead),
                    device_id_type=MESH,
                )

            @pl.when(me >= group - HOPS)
            def _():
                def send_halo(t, carry):
                    for a in (1, 2):
                        halo_in(a, t // group, lax.rem(t, group), me - (group - HOPS)).start()
                    return carry

                lax.fori_loop(0, heads_here * group, send_halo, 0)

        pos = lax.broadcasted_iota(jnp.int32, (rows, 1), 0)

        def zeros_in(which):
            ids = seg[pl.ds(which, 1), :]
            return jnp.sum(jnp.where(ids == 0, 1.0, 0.0), axis=1, keepdims=True).astype(jnp.int32)

        def low_of(b, cut):
            first = (base + b) * rows
            return jnp.where(pos + first >= cut, cut, 0) - first

        def z_copy(h, b, slot):
            return pltpu.make_async_remote_copy(
                src_ref=fb.at[h, rows_of(b)],
                dst_ref=xb.at[h, rows_of(b)],
                send_sem=z_send.at[h, slot],
                recv_sem=z_recv.at[h, slot],
                device_id=(c, ahead),
                device_id_type=MESH,
            )

        own_cut = zeros_in(s)
        start = lax.rem(me + group - HOPS, group)

        def layer_one(t, h):
            i = 2 * t

            @pl.when(i == 0)
            def _():
                for a in range(3):
                    own_copy(a, h).wait()

                def arrived(k, inner):
                    for a in range(3):
                        in_copy(a, h, k, lax.rem(me + group - k, group)).wait_recv()
                    return inner

                lax.fori_loop(1, group, arrived, 0)
                if groups > 1:
                    for a in (1, 2):
                        for j in range(HOPS):
                            halo_in(a, h, j, j).wait_recv()

            tiles = [lax.rem(start + i + j, group) for j in range(2)]
            results = attend_all(
                [
                    (
                        qb[h, rows_of(b)],
                        kb[h, rows_of(b, HOPS + 1)],
                        vb[h, rows_of(b, HOPS + 1)],
                        low_of(b, own_cut),
                    )
                    for b in tiles
                ],
                1.0 / math.sqrt(HD),
                True,
            )
            for j, (b, result) in enumerate(zip(tiles, results)):
                fb[h, rows_of(b)] = result
                z_copy(h, b, i + j).start()
                if groups > 1:
                    @pl.when(b >= group - HOPS)
                    def _():
                        halo_z(h, b - (group - HOPS), b).start()
            return h

        prior_cut = zeros_in(behind)

        def normalize(x):
            x = x.astype(jnp.float32)
            mean = jnp.mean(x * x, axis=1, keepdims=True)
            return (x * lax.rsqrt(mean + 1e-06)).astype(jnp.bfloat16)

        def gained(normed, gain, h):
            g = gain[:, cols_of(me, h)].astype(jnp.float32)
            return (normed.astype(jnp.float32) * g).astype(jnp.bfloat16)

        def take(h, slot):
            b = lax.rem(start + slot, group)
            z_copy(h, b, slot).wait_recv()
            normed = normalize(xb[h, rows_of(b)])
            nb[h, rows_of(b + HOPS)] = normed
            k2b[h, rows_of(b + HOPS)] = gained(normed, gk, h)

        def out_copy(h, k):
            return pltpu.make_async_remote_copy(
                src_ref=ob.at[h, rows_of(lax.rem(me + k, group))],
                dst_ref=out.at[0, :, cols_of(me, h)],
                send_sem=o_send.at[h, k],
                recv_sem=o_recv.at[h, k],
                device_id=(peer(k), s),
                device_id_type=MESH,
            )

        def out_own(h):
            return pltpu.make_async_copy(
                ob.at[h, rows_of(me)], out.at[0, :, cols_of(me, h)], o_recv.at[h, 0]
            )

        def layer_two(t, h):
            i = 2 * t

            @pl.when(i == 0)
            def _():
                if groups > 1:
                    for j in range(HOPS):
                        halo_z(h, j, j).wait_recv()
                        normed = normalize(nb[h, rows_of(j)])
                        nb[h, rows_of(j)] = normed
                        k2b[h, rows_of(j)] = gained(normed, gk, h)

                def first_ones(slot, inner):
                    take(h, slot)
                    return inner

                lax.fori_loop(0, HOPS, first_ones, 0)

            for j in range(2):
                @pl.when(i + j < group - HOPS)
                def _():
                    take(h, i + j + HOPS)

            tiles = [lax.rem(me + i + j, group) for j in range(2)]
            normed = [nb[h, rows_of(b + HOPS)] for b in tiles]
            results = attend_all(
                [
                    (
                        gained(own, gq, h),
                        k2b[h, rows_of(b, HOPS + 1)],
                        nb[h, rows_of(b, HOPS + 1)],
                        low_of(b, prior_cut),
                    )
                    for b, own in zip(tiles, normed)
                ],
                1.0 / HD,
                False,
            )
            for b, own, second in zip(tiles, normed, results):
                mixed = second.astype(jnp.float32) + own.astype(jnp.float32)
                ob[h, rows_of(b)] = mixed.astype(jnp.bfloat16)

            @pl.when(i == 0)
            def _():
                out_own(h).start()

            @pl.when(i > 0)
            def _():
                out_copy(h, i).start()

            out_copy(h, i + 1).start()
            return h

        def both_layers(h, carry):
            lax.fori_loop(0, half, layer_one, h)
            lax.fori_loop(0, half, layer_two, h)
            return carry

        lax.fori_loop(0, heads_here, both_layers, 0)

        def finish(t, carry):
            h = t // (group - 1)
            k = 1 + lax.rem(t, group - 1)
            @pl.when(h == heads_here - 1)
            def _():
                for a in range(3):
                    in_copy(a, h, k, me).wait_send()

            out_copy(h, k).wait_send()
            p = lax.rem(me + group - k, group)
            pltpu.make_async_remote_copy(
                src_ref=ob.at[h, rows_of(me)],
                dst_ref=out.at[0, :, cols_of(p, h)],
                send_sem=o_send.at[h, k],
                recv_sem=o_recv.at[h, k],
                device_id=(peer(k), s),
                device_id_type=MESH,
            ).wait_recv()
            return carry

        lax.fori_loop(0, heads_here * (group - 1), finish, 0)

        def finish_z(t, carry):
            h = t // group
            i = lax.rem(t, group)
            z_copy(h, lax.rem(start + i, group), i).wait_send()
            return carry

        lax.fori_loop(0, heads_here * group, finish_z, 0)
        for h in range(heads_here):
            out_own(h).wait()
            if groups > 1:
                for j in range(HOPS):
                    halo_z(h, j, group - HOPS + j).wait_send()
        if groups > 1:
            @pl.when(me >= group - HOPS)
            def _():
                def sent_halo(t, carry):
                    for a in (1, 2):
                        halo_in(a, t // group, lax.rem(t, group), me - (group - HOPS)).wait_send()
                    return carry

                lax.fori_loop(0, heads_here * group, sent_halo, 0)

    return kernel


def solution(mesh):
    ctx = mesh.shape["ctx"]
    sections = mesh.shape["section"]
    group = math.gcd(ctx, 8)

    def per_device(queries, keys, values, segments, gain_query, gain_key):
        _, rows, width = queries.shape
        heads_here = width // HD // group
        padded = (group + HOPS) * rows
        bf = jnp.bfloat16
        dma = pltpu.SemaphoreType.DMA
        scratch = [
            pltpu.VMEM((heads_here, group * rows, HD), bf),
            pltpu.VMEM((heads_here, padded, HD), bf),
            pltpu.VMEM((heads_here, padded, HD), bf),
            pltpu.VMEM((heads_here, group * rows, HD), bf),
            pltpu.VMEM((heads_here, group * rows, HD), bf),
            pltpu.VMEM((heads_here, padded, HD), bf),
            pltpu.VMEM((heads_here, padded, HD), bf),
            pltpu.VMEM((heads_here, group * rows, HD), bf),
            pltpu.VMEM(segments.shape, segments.dtype),
            pltpu.VMEM(gain_query.shape, bf),
            pltpu.VMEM(gain_key.shape, bf),
            dma((3,)),
            dma((3, heads_here, group)),
            dma((3, heads_here, group)),
            dma((heads_here, group)),
            dma((heads_here, group)),
            dma((heads_here, group)),
            dma((heads_here, group)),
        ]
        if ctx > group:
            scratch += [
                dma((2, heads_here, group)),
                dma((2, heads_here, HOPS)),
                dma((heads_here, HOPS)),
                dma((heads_here, HOPS)),
            ]
        return pl.pallas_call(
            make_kernel(ctx, sections, group, rows, heads_here),
            out_shape=jax.ShapeDtypeStruct(queries.shape, bf),
            in_specs=[pl.BlockSpec(memory_space=pltpu.HBM)] * 6,
            out_specs=pl.BlockSpec(memory_space=pl.ANY),
            scratch_shapes=scratch,
            compiler_params=pltpu.CompilerParams(
                collective_id=0, has_side_effects=True, vmem_limit_bytes=60 * 1024 * 1024
            ),
        )(queries, keys, values, segments, gain_query, gain_key)

    return jax.shard_map(
        per_device,
        mesh=mesh,
        in_specs=(
            P("section", "ctx", None),
            P("section", "ctx", None),
            P("section", "ctx", None),
            P(),
            P("section", None),
            P("section", None),
        ),
        out_specs=P("section", "ctx", None),
        check_vma=False,
    )
```

```python
import math

import jax
import jax.numpy as jnp
from jax import lax
from jax.experimental import pallas as pl
from jax.experimental.pallas import tpu as pltpu
from jax.sharding import PartitionSpec as P

HD = 128
HOPS = 3
NEG = -1e30
LOG2E = 1.4426950408889634
MESH = pl.DeviceIdType.MESH


def score_of(q, k):
    return lax.dot_general(q, k, (((1,), (1,)), ((), ())), preferred_element_type=jnp.float32)


def weights_of(s, low, scale, shift):
    rows = s.shape[0]
    row = lax.broadcasted_iota(jnp.int32, (rows, rows), 0)
    col = lax.broadcasted_iota(jnp.int32, (rows, rows), 1)
    new = col <= row
    place = jnp.where(new, col, col - HOPS * rows)
    merged = jnp.where(new, s[:, HOPS * rows :], s[:, :rows])
    parts = [jnp.where(place >= low, merged, NEG)]
    for j in range(1, HOPS):
        parts.append(jnp.where(col + (j - HOPS) * rows >= low, s[:, j * rows : (j + 1) * rows], NEG))
    if shift:
        top = parts[0]
        for part in parts[1:]:
            top = jnp.maximum(top, part)
        m = jnp.max(top, axis=1, keepdims=True)
        parts = [part - m for part in parts]
    probs = [jnp.exp2(part * (scale * LOG2E)) for part in parts]
    total = probs[0]
    for prob in probs[1:]:
        total = total + prob
    l = jnp.sum(total, axis=1, keepdims=True)
    old_p = jnp.where(new, 0.0, probs[0]).astype(jnp.bfloat16)
    new_p = jnp.where(new, probs[0], 0.0).astype(jnp.bfloat16)
    return jnp.concatenate([old_p] + [x.astype(jnp.bfloat16) for x in probs[1:]] + [new_p], axis=1), l


def attend_all(tiles, scale, shift):
    scores = [score_of(q, k) for q, k, _, _ in tiles]
    outs = []
    for s, (_, _, v, low) in zip(scores, tiles):
        pb, l = weights_of(s, low, scale, shift)
        out = jnp.dot(pb, v, preferred_element_type=jnp.float32)
        outs.append((out / l).astype(jnp.bfloat16))
    return outs


def make_kernel(ctx, sections, group, rows, heads_here):
    groups = ctx // group
    pad = HOPS * rows
    width = heads_here * HD

    def kernel(q_in, k_in, v_in, seg_in, gq_in, gk_in, out, qb, kb, vb, fb, xb, nb, k2b, ob, seg, gq, gk,
               small, in_send, in_recv, z_send, z_recv, o_send, o_recv, *halo):
        c = lax.axis_index("ctx")
        s = lax.axis_index("section")
        grp = c // group
        me = c % group
        base = grp * group
        ahead = lax.rem(s + 1, sections)
        behind = lax.rem(s + sections - 1, sections)
        next_base = lax.rem(grp + 1, groups) * group
        prev_base = lax.rem(grp + groups - 1, groups) * group

        def rows_of(b, count=1):
            return pl.ds(pl.multiple_of(b * rows, rows), count * rows)

        def peer(k):
            return base + lax.rem(me + k, group)

        def cols_of(p, h):
            return pl.ds(pl.multiple_of(lax.rem(p, group) * width + h * HD, HD), HD)

        barrier = pltpu.get_barrier_semaphore()

        def greet(k, carry):
            pl.semaphore_signal(barrier, inc=1, device_id=(peer(k), s), device_id_type=MESH)
            return carry

        lax.fori_loop(1, group, greet, 0)
        pl.semaphore_signal(barrier, inc=1, device_id=(c, ahead), device_id_type=MESH)
        pl.semaphore_signal(barrier, inc=1, device_id=(c, behind), device_id_type=MESH)
        expected = group + 1
        if groups > 1:
            def greet_far(k, carry):
                pl.semaphore_signal(barrier, inc=1, device_id=(next_base + k, s), device_id_type=MESH)
                pl.semaphore_signal(barrier, inc=1, device_id=(prev_base + k, s), device_id_type=MESH)
                return carry

            lax.fori_loop(0, group, greet_far, 0)
            pl.semaphore_signal(barrier, inc=1, device_id=(next_base + me, ahead), device_id_type=MESH)
            pl.semaphore_signal(barrier, inc=1, device_id=(prev_base + me, behind), device_id_type=MESH)
            expected = expected + 2 * group + 2

        ins = (q_in, k_in, v_in)
        bufs = (qb, kb, vb)
        lead = (0, HOPS, HOPS)

        def own_copy(a, h):
            return pltpu.make_async_copy(
                ins[a].at[0, :, cols_of(me, h)], bufs[a].at[h, rows_of(me + lead[a])], in_recv.at[a, h, 0]
            )

        def in_copy(a, h, k, place):
            p = peer(k)
            return pltpu.make_async_remote_copy(
                src_ref=ins[a].at[0, :, cols_of(p, h)],
                dst_ref=bufs[a].at[h, rows_of(place + lead[a])],
                send_sem=in_send.at[a, h, k],
                recv_sem=in_recv.at[a, h, k],
                device_id=(p, s),
                device_id_type=MESH,
            )

        smalls = [
            pltpu.make_async_copy(src, dst, small.at[j])
            for j, (src, dst) in enumerate(((seg_in, seg), (gq_in, gq), (gk_in, gk)))
        ]
        for copy in smalls:
            copy.start()
        for h in range(heads_here):
            for a in range(3):
                own_copy(a, h).start()
        if groups == 1:
            zero = jnp.zeros((heads_here, pad, HD), jnp.bfloat16)
            kb[:, :pad, :] = zero
            vb[:, :pad, :] = zero
            k2b[:, :pad, :] = zero
            nb[:, :pad, :] = zero
        pl.semaphore_wait(barrier, expected)

        half = group // 2

        def send_in(t, carry):
            h = t // group
            k = lax.rem(t // half + me, 2) + 2 * lax.rem(t, half)

            @pl.when(k > 0)
            def _():
                for a in range(3):
                    in_copy(a, h, k, me).start()

            return carry

        lax.fori_loop(0, heads_here * group, send_in, 0)
        for copy in smalls:
            copy.wait()

        if groups > 1:
            hi_send, hi_recv, hz_send, hz_recv = halo

            def halo_in(a, h, k, j):
                return pltpu.make_async_remote_copy(
                    src_ref=ins[a].at[0, :, cols_of(k, h)],
                    dst_ref=bufs[a].at[h, rows_of(j)],
                    send_sem=hi_send.at[a - 1, h, k],
                    recv_sem=hi_recv.at[a - 1, h, j],
                    device_id=(next_base + k, s),
                    device_id_type=MESH,
                )

            def halo_z(h, j, b):
                return pltpu.make_async_remote_copy(
                    src_ref=fb.at[h, rows_of(b)],
                    dst_ref=nb.at[h, rows_of(j)],
                    send_sem=hz_send.at[h, j],
                    recv_sem=hz_recv.at[h, j],
                    device_id=(next_base + me, ahead),
                    device_id_type=MESH,
                )

            @pl.when(me >= group - HOPS)
            def _():
                def send_halo(t, carry):
                    for a in (1, 2):
                        halo_in(a, t // group, lax.rem(t, group), me - (group - HOPS)).start()
                    return carry

                lax.fori_loop(0, heads_here * group, send_halo, 0)

        pos = lax.broadcasted_iota(jnp.int32, (rows, 1), 0)

        def zeros_in(which):
            ids = seg[pl.ds(which, 1), :]
            return jnp.sum(jnp.where(ids == 0, 1.0, 0.0), axis=1, keepdims=True).astype(jnp.int32)

        def low_of(b, cut):
            first = (base + b) * rows
            return jnp.where(pos + first >= cut, cut, 0) - first

        def z_copy(h, b, slot):
            return pltpu.make_async_remote_copy(
                src_ref=fb.at[h, rows_of(b)],
                dst_ref=xb.at[h, rows_of(b)],
                send_sem=z_send.at[h, slot],
                recv_sem=z_recv.at[h, slot],
                device_id=(c, ahead),
                device_id_type=MESH,
            )

        own_cut = zeros_in(s)
        start = lax.rem(me + group - HOPS, group)

        def layer_one(t, h):
            i = 2 * t

            @pl.when(i == 0)
            def _():
                for a in range(3):
                    own_copy(a, h).wait()

                def arrived(k, inner):
                    for a in range(3):
                        in_copy(a, h, k, lax.rem(me + group - k, group)).wait_recv()
                    return inner

                lax.fori_loop(1, group, arrived, 0)
                if groups > 1:
                    for a in (1, 2):
                        for j in range(HOPS):
                            halo_in(a, h, j, j).wait_recv()

            tiles = [lax.rem(start + i + j, group) for j in range(2)]
            results = attend_all(
                [
                    (
                        qb[h, rows_of(b)],
                        kb[h, rows_of(b, HOPS + 1)],
                        vb[h, rows_of(b, HOPS + 1)],
                        low_of(b, own_cut),
                    )
                    for b in tiles
                ],
                1.0 / math.sqrt(HD),
                True,
            )
            for j, (b, result) in enumerate(zip(tiles, results)):
                fb[h, rows_of(b)] = result
                z_copy(h, b, i + j).start()
                if groups > 1:
                    @pl.when(b >= group - HOPS)
                    def _():
                        halo_z(h, b - (group - HOPS), b).start()
            return h

        prior_cut = zeros_in(behind)

        def normalize(x):
            x = x.astype(jnp.float32)
            mean = jnp.mean(x * x, axis=1, keepdims=True)
            return (x * lax.rsqrt(mean + 1e-06)).astype(jnp.bfloat16)

        def gained(normed, gain, h):
            g = gain[:, cols_of(me, h)].astype(jnp.float32)
            return (normed.astype(jnp.float32) * g).astype(jnp.bfloat16)

        def take(h, slot):
            b = lax.rem(start + slot, group)
            z_copy(h, b, slot).wait_recv()
            normed = normalize(xb[h, rows_of(b)])
            nb[h, rows_of(b + HOPS)] = normed
            k2b[h, rows_of(b + HOPS)] = gained(normed, gk, h)

        def out_copy(h, k):
            return pltpu.make_async_remote_copy(
                src_ref=ob.at[h, rows_of(lax.rem(me + k, group))],
                dst_ref=out.at[0, :, cols_of(me, h)],
                send_sem=o_send.at[h, k],
                recv_sem=o_recv.at[h, k],
                device_id=(peer(k), s),
                device_id_type=MESH,
            )

        def out_own(h):
            return pltpu.make_async_copy(
                ob.at[h, rows_of(me)], out.at[0, :, cols_of(me, h)], o_recv.at[h, 0]
            )

        def layer_two(t, h):
            i = 2 * t

            @pl.when(i == 0)
            def _():
                if groups > 1:
                    for j in range(HOPS):
                        halo_z(h, j, j).wait_recv()
                        normed = normalize(nb[h, rows_of(j)])
                        nb[h, rows_of(j)] = normed
                        k2b[h, rows_of(j)] = gained(normed, gk, h)

                def first_ones(slot, inner):
                    take(h, slot)
                    return inner

                lax.fori_loop(0, HOPS, first_ones, 0)

            for j in range(2):
                @pl.when(i + j < group - HOPS)
                def _():
                    take(h, i + j + HOPS)

            tiles = [lax.rem(me + i + j, group) for j in range(2)]
            normed = [nb[h, rows_of(b + HOPS)] for b in tiles]
            results = attend_all(
                [
                    (
                        gained(own, gq, h),
                        k2b[h, rows_of(b, HOPS + 1)],
                        nb[h, rows_of(b, HOPS + 1)],
                        low_of(b, prior_cut),
                    )
                    for b, own in zip(tiles, normed)
                ],
                1.0 / HD,
                False,
            )
            for b, own, second in zip(tiles, normed, results):
                mixed = second.astype(jnp.float32) + own.astype(jnp.float32)
                ob[h, rows_of(b)] = mixed.astype(jnp.bfloat16)

            @pl.when(i == 0)
            def _():
                out_own(h).start()

            @pl.when(i > 0)
            def _():
                out_copy(h, i).start()

            out_copy(h, i + 1).start()
            return h

        def all_tiles(layer):
            def one_head(h, carry):
                lax.fori_loop(0, half, layer, h)
                return carry

            lax.fori_loop(0, heads_here, one_head, 0)

        all_tiles(layer_one)
        all_tiles(layer_two)

        def finish(t, carry):
            h = t // (group - 1)
            k = 1 + lax.rem(t, group - 1)
            for a in range(3):
                in_copy(a, h, k, me).wait_send()
            out_copy(h, k).wait_send()
            p = lax.rem(me + group - k, group)
            pltpu.make_async_remote_copy(
                src_ref=ob.at[h, rows_of(me)],
                dst_ref=out.at[0, :, cols_of(p, h)],
                send_sem=o_send.at[h, k],
                recv_sem=o_recv.at[h, k],
                device_id=(peer(k), s),
                device_id_type=MESH,
            ).wait_recv()
            return carry

        lax.fori_loop(0, heads_here * (group - 1), finish, 0)

        def finish_z(t, carry):
            h = t // group
            i = lax.rem(t, group)
            z_copy(h, lax.rem(start + i, group), i).wait_send()
            return carry

        lax.fori_loop(0, heads_here * group, finish_z, 0)
        for h in range(heads_here):
            out_own(h).wait()
            if groups > 1:
                for j in range(HOPS):
                    halo_z(h, j, group - HOPS + j).wait_send()
        if groups > 1:
            @pl.when(me >= group - HOPS)
            def _():
                def sent_halo(t, carry):
                    for a in (1, 2):
                        halo_in(a, t // group, lax.rem(t, group), me - (group - HOPS)).wait_send()
                    return carry

                lax.fori_loop(0, heads_here * group, sent_halo, 0)

    return kernel


def solution(mesh):
    ctx = mesh.shape["ctx"]
    sections = mesh.shape["section"]
    group = math.gcd(ctx, 8)

    def per_device(queries, keys, values, segments, gain_query, gain_key):
        _, rows, width = queries.shape
        heads_here = width // HD // group
        padded = (group + HOPS) * rows
        bf = jnp.bfloat16
        dma = pltpu.SemaphoreType.DMA
        scratch = [
            pltpu.VMEM((heads_here, group * rows, HD), bf),
            pltpu.VMEM((heads_here, padded, HD), bf),
            pltpu.VMEM((heads_here, padded, HD), bf),
            pltpu.VMEM((heads_here, group * rows, HD), bf),
            pltpu.VMEM((heads_here, group * rows, HD), bf),
            pltpu.VMEM((heads_here, padded, HD), bf),
            pltpu.VMEM((heads_here, padded, HD), bf),
            pltpu.VMEM((heads_here, group * rows, HD), bf),
            pltpu.VMEM(segments.shape, segments.dtype),
            pltpu.VMEM(gain_query.shape, bf),
            pltpu.VMEM(gain_key.shape, bf),
            dma((3,)),
            dma((3, heads_here, group)),
            dma((3, heads_here, group)),
            dma((heads_here, group)),
            dma((heads_here, group)),
            dma((heads_here, group)),
            dma((heads_here, group)),
        ]
        if ctx > group:
            scratch += [
                dma((2, heads_here, group)),
                dma((2, heads_here, HOPS)),
                dma((heads_here, HOPS)),
                dma((heads_here, HOPS)),
            ]
        return pl.pallas_call(
            make_kernel(ctx, sections, group, rows, heads_here),
            out_shape=jax.ShapeDtypeStruct(queries.shape, bf),
            in_specs=[pl.BlockSpec(memory_space=pltpu.HBM)] * 6,
            out_specs=pl.BlockSpec(memory_space=pl.ANY),
            scratch_shapes=scratch,
            compiler_params=pltpu.CompilerParams(
                collective_id=0, has_side_effects=True, vmem_limit_bytes=60 * 1024 * 1024
            ),
        )(queries, keys, values, segments, gain_query, gain_key)

    return jax.shard_map(
        per_device,
        mesh=mesh,
        in_specs=(
            P("section", "ctx", None),
            P("section", "ctx", None),
            P("section", "ctx", None),
            P(),
            P("section", None),
            P("section", None),
        ),
        out_specs=P("section", "ctx", None),
        check_vma=False,
    )
```

```python
import math

import jax
import jax.numpy as jnp
from jax import lax
from jax.experimental import pallas as pl
from jax.experimental.pallas import tpu as pltpu
from jax.sharding import PartitionSpec as P

HD = 128
HOPS = 3
NEG = -1e30
LOG2E = 1.4426950408889634
MESH = pl.DeviceIdType.MESH


def score_of(q, k):
    return lax.dot_general(q, k, (((1,), (1,)), ((), ())), preferred_element_type=jnp.float32)


def weights_of(s, low, scale, shift):
    rows = s.shape[0]
    row = lax.broadcasted_iota(jnp.int32, (rows, rows), 0)
    col = lax.broadcasted_iota(jnp.int32, (rows, rows), 1)
    new = col <= row
    place = jnp.where(new, col, col - HOPS * rows)
    merged = jnp.where(new, s[:, HOPS * rows :], s[:, :rows])
    parts = [jnp.where(place >= low, merged, NEG)]
    for j in range(1, HOPS):
        parts.append(jnp.where(col + (j - HOPS) * rows >= low, s[:, j * rows : (j + 1) * rows], NEG))
    if shift:
        top = parts[0]
        for part in parts[1:]:
            top = jnp.maximum(top, part)
        m = jnp.max(top, axis=1, keepdims=True)
        parts = [part - m for part in parts]
    probs = [jnp.exp2(part * (scale * LOG2E)) for part in parts]
    total = probs[0]
    for prob in probs[1:]:
        total = total + prob
    l = jnp.sum(total, axis=1, keepdims=True)
    old_p = jnp.where(new, 0.0, probs[0]).astype(jnp.bfloat16)
    new_p = jnp.where(new, probs[0], 0.0).astype(jnp.bfloat16)
    return jnp.concatenate([old_p] + [x.astype(jnp.bfloat16) for x in probs[1:]] + [new_p], axis=1), l


def attend_all(tiles, scale, shift):
    scores = [score_of(q, k) for q, k, _, _ in tiles]
    outs = []
    for s, (_, _, v, low) in zip(scores, tiles):
        pb, l = weights_of(s, low, scale, shift)
        out = jnp.dot(pb, v, preferred_element_type=jnp.float32)
        outs.append((out / l).astype(jnp.bfloat16))
    return outs


def make_kernel(ctx, sections, group, rows, heads_here):
    groups = ctx // group
    pad = HOPS * rows
    width = heads_here * HD

    def kernel(q_in, k_in, v_in, seg_in, gq_in, gk_in, out, qb, kb, vb, fb, xb, nb, k2b, ob, seg, gq, gk,
               small, in_send, in_recv, z_send, z_recv, o_send, o_recv, *halo):
        c = lax.axis_index("ctx")
        s = lax.axis_index("section")
        grp = c // group
        me = c % group
        base = grp * group
        ahead = lax.rem(s + 1, sections)
        behind = lax.rem(s + sections - 1, sections)
        next_base = lax.rem(grp + 1, groups) * group
        prev_base = lax.rem(grp + groups - 1, groups) * group

        def rows_of(b, count=1):
            return pl.ds(pl.multiple_of(b * rows, rows), count * rows)

        def peer(k):
            return base + lax.rem(me + k, group)

        def cols_of(p, h):
            return pl.ds(pl.multiple_of(lax.rem(p, group) * width + h * HD, HD), HD)

        barrier = pltpu.get_barrier_semaphore()

        def greet(k, carry):
            pl.semaphore_signal(barrier, inc=1, device_id=(peer(k), s), device_id_type=MESH)
            return carry

        lax.fori_loop(1, group, greet, 0)
        pl.semaphore_signal(barrier, inc=1, device_id=(c, ahead), device_id_type=MESH)
        pl.semaphore_signal(barrier, inc=1, device_id=(c, behind), device_id_type=MESH)
        expected = group + 1
        if groups > 1:
            def greet_far(k, carry):
                pl.semaphore_signal(barrier, inc=1, device_id=(next_base + k, s), device_id_type=MESH)
                pl.semaphore_signal(barrier, inc=1, device_id=(prev_base + k, s), device_id_type=MESH)
                return carry

            lax.fori_loop(0, group, greet_far, 0)
            pl.semaphore_signal(barrier, inc=1, device_id=(next_base + me, ahead), device_id_type=MESH)
            pl.semaphore_signal(barrier, inc=1, device_id=(prev_base + me, behind), device_id_type=MESH)
            expected = expected + 2 * group + 2

        ins = (q_in, k_in, v_in)
        bufs = (qb, kb, vb)
        lead = (0, HOPS, HOPS)

        def own_copy(a, h):
            return pltpu.make_async_copy(
                ins[a].at[0, :, cols_of(me, h)], bufs[a].at[h, rows_of(me + lead[a])], in_recv.at[a, h, 0]
            )

        def in_copy(a, h, k, place):
            p = peer(k)
            return pltpu.make_async_remote_copy(
                src_ref=ins[a].at[0, :, cols_of(p, h)],
                dst_ref=bufs[a].at[h, rows_of(place + lead[a])],
                send_sem=in_send.at[a, h, k],
                recv_sem=in_recv.at[a, h, k],
                device_id=(p, s),
                device_id_type=MESH,
            )

        smalls = [
            pltpu.make_async_copy(src, dst, small.at[j])
            for j, (src, dst) in enumerate(((seg_in, seg), (gq_in, gq), (gk_in, gk)))
        ]
        for copy in smalls:
            copy.start()
        for h in range(heads_here):
            for a in range(3):
                own_copy(a, h).start()
        if groups == 1:
            zero = jnp.zeros((heads_here, pad, HD), jnp.bfloat16)
            kb[:, :pad, :] = zero
            vb[:, :pad, :] = zero
            k2b[:, :pad, :] = zero
            nb[:, :pad, :] = zero
        pl.semaphore_wait(barrier, expected)

        half = group // 2

        def send_in(t, carry):
            h = t // group
            k = lax.rem(t // half + me, 2) + 2 * lax.rem(t, half)

            @pl.when(k > 0)
            def _():
                for a in range(3):
                    in_copy(a, h, k, me).start()

            return carry

        lax.fori_loop(0, heads_here * group, send_in, 0)
        for copy in smalls:
            copy.wait()

        if groups > 1:
            hi_send, hi_recv, hz_send, hz_recv = halo

            def halo_in(a, h, k, j):
                return pltpu.make_async_remote_copy(
                    src_ref=ins[a].at[0, :, cols_of(k, h)],
                    dst_ref=bufs[a].at[h, rows_of(j)],
                    send_sem=hi_send.at[a - 1, h, k],
                    recv_sem=hi_recv.at[a - 1, h, j],
                    device_id=(next_base + k, s),
                    device_id_type=MESH,
                )

            def halo_z(h, j, b):
                return pltpu.make_async_remote_copy(
                    src_ref=fb.at[h, rows_of(b)],
                    dst_ref=nb.at[h, rows_of(j)],
                    send_sem=hz_send.at[h, j],
                    recv_sem=hz_recv.at[h, j],
                    device_id=(next_base + me, ahead),
                    device_id_type=MESH,
                )

            @pl.when(me >= group - HOPS)
            def _():
                def send_halo(t, carry):
                    for a in (1, 2):
                        halo_in(a, t // group, lax.rem(t, group), me - (group - HOPS)).start()
                    return carry

                lax.fori_loop(0, heads_here * group, send_halo, 0)

        pos = lax.broadcasted_iota(jnp.int32, (rows, 1), 0)

        def zeros_in(which):
            ids = seg[pl.ds(which, 1), :]
            return jnp.sum(jnp.where(ids == 0, 1.0, 0.0), axis=1, keepdims=True).astype(jnp.int32)

        def low_of(b, cut):
            first = (base + b) * rows
            return jnp.where(pos + first >= cut, cut, 0) - first

        def z_copy(h, b, slot):
            return pltpu.make_async_remote_copy(
                src_ref=fb.at[h, rows_of(b)],
                dst_ref=xb.at[h, rows_of(b)],
                send_sem=z_send.at[h, slot],
                recv_sem=z_recv.at[h, slot],
                device_id=(c, ahead),
                device_id_type=MESH,
            )

        own_cut = zeros_in(s)
        start = lax.rem(me + group - HOPS, group)

        def layer_one(t, h):
            i = 2 * t

            @pl.when(i == 0)
            def _():
                for a in range(3):
                    own_copy(a, h).wait()

                def arrived(k, inner):
                    for a in range(3):
                        in_copy(a, h, k, lax.rem(me + group - k, group)).wait_recv()
                    return inner

                lax.fori_loop(1, group, arrived, 0)
                if groups > 1:
                    for a in (1, 2):
                        for j in range(HOPS):
                            halo_in(a, h, j, j).wait_recv()

            tiles = [lax.rem(start + i + j, group) for j in range(2)]
            results = attend_all(
                [
                    (
                        qb[h, rows_of(b)],
                        kb[h, rows_of(b, HOPS + 1)],
                        vb[h, rows_of(b, HOPS + 1)],
                        low_of(b, own_cut),
                    )
                    for b in tiles
                ],
                1.0 / math.sqrt(HD),
                True,
            )
            for j, (b, result) in enumerate(zip(tiles, results)):
                fb[h, rows_of(b)] = result
                z_copy(h, b, i + j).start()
                if groups > 1:
                    @pl.when(b >= group - HOPS)
                    def _():
                        halo_z(h, b - (group - HOPS), b).start()
            return h

        prior_cut = zeros_in(behind)

        def normalize(x):
            x = x.astype(jnp.float32)
            mean = jnp.mean(x * x, axis=1, keepdims=True)
            return (x * lax.rsqrt(mean + 1e-06)).astype(jnp.bfloat16)

        def gained(normed, gain, h):
            g = gain[:, cols_of(me, h)].astype(jnp.float32)
            return (normed.astype(jnp.float32) * g).astype(jnp.bfloat16)

        def take(h, slot):
            b = lax.rem(start + slot, group)
            z_copy(h, b, slot).wait_recv()
            normed = normalize(xb[h, rows_of(b)])
            nb[h, rows_of(b + HOPS)] = normed
            k2b[h, rows_of(b + HOPS)] = gained(normed, gk, h)

        def out_copy(h, k):
            return pltpu.make_async_remote_copy(
                src_ref=ob.at[h, rows_of(lax.rem(me + k, group))],
                dst_ref=out.at[0, :, cols_of(me, h)],
                send_sem=o_send.at[h, k],
                recv_sem=o_recv.at[h, k],
                device_id=(peer(k), s),
                device_id_type=MESH,
            )

        def out_own(h):
            return pltpu.make_async_copy(
                ob.at[h, rows_of(me)], out.at[0, :, cols_of(me, h)], o_recv.at[h, 0]
            )

        def layer_two(t, h):
            i = 2 * t

            @pl.when(i == 0)
            def _():
                if groups > 1:
                    for j in range(HOPS):
                        halo_z(h, j, j).wait_recv()
                        normed = normalize(nb[h, rows_of(j)])
                        nb[h, rows_of(j)] = normed
                        k2b[h, rows_of(j)] = gained(normed, gk, h)

                def first_ones(slot, inner):
                    take(h, slot)
                    return inner

                lax.fori_loop(0, HOPS, first_ones, 0)

            for j in range(2):
                @pl.when(i + j < group - HOPS)
                def _():
                    take(h, i + j + HOPS)

            tiles = [lax.rem(me + i + j, group) for j in range(2)]
            normed = [nb[h, rows_of(b + HOPS)] for b in tiles]
            results = attend_all(
                [
                    (
                        gained(own, gq, h),
                        k2b[h, rows_of(b, HOPS + 1)],
                        nb[h, rows_of(b, HOPS + 1)],
                        low_of(b, prior_cut),
                    )
                    for b, own in zip(tiles, normed)
                ],
                1.0 / HD,
                False,
            )
            for b, own, second in zip(tiles, normed, results):
                mixed = second.astype(jnp.float32) + own.astype(jnp.float32)
                ob[h, rows_of(b)] = mixed.astype(jnp.bfloat16)

            @pl.when(i == 0)
            def _():
                out_own(h).start()

            @pl.when(i > 0)
            def _():
                out_copy(h, i).start()

            out_copy(h, i + 1).start()
            return h

        def both_layers(h, carry):
            lax.fori_loop(0, half, layer_one, h)
            lax.fori_loop(0, half, layer_two, h)
            return carry

        lax.fori_loop(0, heads_here, both_layers, 0)

        def finish(t, carry):
            h = t // (group - 1)
            k = 1 + lax.rem(t, group - 1)
            for a in range(3):
                in_copy(a, h, k, me).wait_send()
            out_copy(h, k).wait_send()
            p = lax.rem(me + group - k, group)
            pltpu.make_async_remote_copy(
                src_ref=ob.at[h, rows_of(me)],
                dst_ref=out.at[0, :, cols_of(p, h)],
                send_sem=o_send.at[h, k],
                recv_sem=o_recv.at[h, k],
                device_id=(peer(k), s),
                device_id_type=MESH,
            ).wait_recv()
            return carry

        lax.fori_loop(0, heads_here * (group - 1), finish, 0)

        def finish_z(t, carry):
            h = t // group
            i = lax.rem(t, group)
            z_copy(h, lax.rem(start + i, group), i).wait_send()
            return carry

        lax.fori_loop(0, heads_here * group, finish_z, 0)
        for h in range(heads_here):
            out_own(h).wait()
            if groups > 1:
                for j in range(HOPS):
                    halo_z(h, j, group - HOPS + j).wait_send()
        if groups > 1:
            @pl.when(me >= group - HOPS)
            def _():
                def sent_halo(t, carry):
                    for a in (1, 2):
                        halo_in(a, t // group, lax.rem(t, group), me - (group - HOPS)).wait_send()
                    return carry

                lax.fori_loop(0, heads_here * group, sent_halo, 0)

    return kernel


def solution(mesh):
    ctx = mesh.shape["ctx"]
    sections = mesh.shape["section"]
    group = math.gcd(ctx, 8)

    def per_device(queries, keys, values, segments, gain_query, gain_key):
        _, rows, width = queries.shape
        heads_here = width // HD // group
        padded = (group + HOPS) * rows
        bf = jnp.bfloat16
        dma = pltpu.SemaphoreType.DMA
        scratch = [
            pltpu.VMEM((heads_here, group * rows, HD), bf),
            pltpu.VMEM((heads_here, padded, HD), bf),
            pltpu.VMEM((heads_here, padded, HD), bf),
            pltpu.VMEM((heads_here, group * rows, HD), bf),
            pltpu.VMEM((heads_here, group * rows, HD), bf),
            pltpu.VMEM((heads_here, padded, HD), bf),
            pltpu.VMEM((heads_here, padded, HD), bf),
            pltpu.VMEM((heads_here, group * rows, HD), bf),
            pltpu.VMEM(segments.shape, segments.dtype),
            pltpu.VMEM(gain_query.shape, bf),
            pltpu.VMEM(gain_key.shape, bf),
            dma((3,)),
            dma((3, heads_here, group)),
            dma((3, heads_here, group)),
            dma((heads_here, group)),
            dma((heads_here, group)),
            dma((heads_here, group)),
            dma((heads_here, group)),
        ]
        if ctx > group:
            scratch += [
                dma((2, heads_here, group)),
                dma((2, heads_here, HOPS)),
                dma((heads_here, HOPS)),
                dma((heads_here, HOPS)),
            ]
        return pl.pallas_call(
            make_kernel(ctx, sections, group, rows, heads_here),
            out_shape=jax.ShapeDtypeStruct(queries.shape, bf),
            in_specs=[pl.BlockSpec(memory_space=pltpu.HBM)] * 6,
            out_specs=pl.BlockSpec(memory_space=pl.ANY),
            scratch_shapes=scratch,
            compiler_params=pltpu.CompilerParams(
                collective_id=0, has_side_effects=True, vmem_limit_bytes=60 * 1024 * 1024
            ),
        )(queries, keys, values, segments, gain_query, gain_key)

    return jax.shard_map(
        per_device,
        mesh=mesh,
        in_specs=(
            P("section", "ctx", None),
            P("section", "ctx", None),
            P("section", "ctx", None),
            P(),
            P("section", None),
            P("section", None),
        ),
        out_specs=P("section", "ctx", None),
        check_vma=False,
    )
```

```python
import math

import jax
import jax.numpy as jnp
from jax import lax
from jax.experimental import pallas as pl
from jax.experimental.pallas import tpu as pltpu
from jax.sharding import PartitionSpec as P

HD = 128
HOPS = 3
NEG = -1e30
LOG2E = 1.4426950408889634
MESH = pl.DeviceIdType.MESH


def score_of(q, k):
    return lax.dot_general(q, k, (((1,), (1,)), ((), ())), preferred_element_type=jnp.float32)


def weights_of(s, low, scale, shift):
    rows = s.shape[0]
    row = lax.broadcasted_iota(jnp.int32, (rows, rows), 0)
    col = lax.broadcasted_iota(jnp.int32, (rows, rows), 1)
    new = col <= row
    place = jnp.where(new, col, col - HOPS * rows)
    merged = jnp.where(new, s[:, HOPS * rows :], s[:, :rows])
    parts = [jnp.where(place >= low, merged, NEG)]
    for j in range(1, HOPS):
        parts.append(jnp.where(col >= low + (HOPS - j) * rows, s[:, j * rows : (j + 1) * rows], NEG))
    if shift:
        top = parts[0]
        for part in parts[1:]:
            top = jnp.maximum(top, part)
        m = jnp.max(top, axis=1, keepdims=True)
        parts = [part - m for part in parts]
    probs = [jnp.exp2(part * (scale * LOG2E)) for part in parts]
    total = probs[0]
    for prob in probs[1:]:
        total = total + prob
    l = jnp.sum(total, axis=1, keepdims=True)
    old_p = jnp.where(new, 0.0, probs[0]).astype(jnp.bfloat16)
    new_p = jnp.where(new, probs[0], 0.0).astype(jnp.bfloat16)
    return jnp.concatenate([old_p] + [x.astype(jnp.bfloat16) for x in probs[1:]] + [new_p], axis=1), l


def attend_all(tiles, scale, shift):
    scores = [score_of(q, k) for q, k, _, _ in tiles]
    outs = []
    for s, (_, _, v, low) in zip(scores, tiles):
        pb, l = weights_of(s, low, scale, shift)
        out = jnp.dot(pb, v, preferred_element_type=jnp.float32)
        outs.append((out / l).astype(jnp.bfloat16))
    return outs


def make_kernel(ctx, sections, group, rows, heads_here):
    groups = ctx // group
    pad = HOPS * rows
    width = heads_here * HD

    def kernel(q_in, k_in, v_in, seg_in, gq_in, gk_in, out, qb, kb, vb, fb, xb, nb, k2b, ob, seg, gq, gk,
               small, in_send, in_recv, z_send, z_recv, o_send, o_recv, *halo):
        c = lax.axis_index("ctx")
        s = lax.axis_index("section")
        grp = c // group
        me = c % group
        base = grp * group
        ahead = lax.rem(s + 1, sections)
        behind = lax.rem(s + sections - 1, sections)
        next_base = lax.rem(grp + 1, groups) * group
        prev_base = lax.rem(grp + groups - 1, groups) * group

        def rows_of(b, count=1):
            return pl.ds(pl.multiple_of(b * rows, rows), count * rows)

        def peer(k):
            return base + lax.rem(me + k, group)

        def cols_of(p, h):
            return pl.ds(pl.multiple_of(lax.rem(p, group) * width + h * HD, HD), HD)

        barrier = pltpu.get_barrier_semaphore()

        def greet(k, carry):
            pl.semaphore_signal(barrier, inc=1, device_id=(peer(k), s), device_id_type=MESH)
            return carry

        lax.fori_loop(1, group, greet, 0)
        pl.semaphore_signal(barrier, inc=1, device_id=(c, ahead), device_id_type=MESH)
        pl.semaphore_signal(barrier, inc=1, device_id=(c, behind), device_id_type=MESH)
        expected = group + 1
        if groups > 1:
            def greet_far(k, carry):
                pl.semaphore_signal(barrier, inc=1, device_id=(next_base + k, s), device_id_type=MESH)
                pl.semaphore_signal(barrier, inc=1, device_id=(prev_base + k, s), device_id_type=MESH)
                return carry

            lax.fori_loop(0, group, greet_far, 0)
            pl.semaphore_signal(barrier, inc=1, device_id=(next_base + me, ahead), device_id_type=MESH)
            pl.semaphore_signal(barrier, inc=1, device_id=(prev_base + me, behind), device_id_type=MESH)
            expected = expected + 2 * group + 2

        ins = (q_in, k_in, v_in)
        bufs = (qb, kb, vb)
        lead = (0, HOPS, HOPS)

        def own_copy(a, h):
            return pltpu.make_async_copy(
                ins[a].at[0, :, cols_of(me, h)], bufs[a].at[h, rows_of(me + lead[a])], in_recv.at[a, h, 0]
            )

        def in_copy(a, h, k, place):
            p = peer(k)
            return pltpu.make_async_remote_copy(
                src_ref=ins[a].at[0, :, cols_of(p, h)],
                dst_ref=bufs[a].at[h, rows_of(place + lead[a])],
                send_sem=in_send.at[a, h, k],
                recv_sem=in_recv.at[a, h, k],
                device_id=(p, s),
                device_id_type=MESH,
            )

        smalls = [
            pltpu.make_async_copy(src, dst, small.at[j])
            for j, (src, dst) in enumerate(((seg_in, seg), (gq_in, gq), (gk_in, gk)))
        ]
        for copy in smalls:
            copy.start()
        for h in range(heads_here):
            for a in range(3):
                own_copy(a, h).start()
        if groups == 1:
            zero = jnp.zeros((heads_here, pad, HD), jnp.bfloat16)
            kb[:, :pad, :] = zero
            vb[:, :pad, :] = zero
            k2b[:, :pad, :] = zero
            nb[:, :pad, :] = zero
        pl.semaphore_wait(barrier, expected)

        half = group // 2

        def send_in(t, carry):
            h = t // group
            k = lax.rem(t // half + me, 2) + 2 * lax.rem(t, half)

            @pl.when(k > 0)
            def _():
                for a in range(3):
                    in_copy(a, h, k, me).start()

            return carry

        lax.fori_loop(0, heads_here * group, send_in, 0)
        for copy in smalls:
            copy.wait()

        if groups > 1:
            hi_send, hi_recv, hz_send, hz_recv = halo

            def halo_in(a, h, k, j):
                return pltpu.make_async_remote_copy(
                    src_ref=ins[a].at[0, :, cols_of(k, h)],
                    dst_ref=bufs[a].at[h, rows_of(j)],
                    send_sem=hi_send.at[a - 1, h, k],
                    recv_sem=hi_recv.at[a - 1, h, j],
                    device_id=(next_base + k, s),
                    device_id_type=MESH,
                )

            def halo_z(h, j, b):
                return pltpu.make_async_remote_copy(
                    src_ref=fb.at[h, rows_of(b)],
                    dst_ref=nb.at[h, rows_of(j)],
                    send_sem=hz_send.at[h, j],
                    recv_sem=hz_recv.at[h, j],
                    device_id=(next_base + me, ahead),
                    device_id_type=MESH,
                )

            @pl.when(me >= group - HOPS)
            def _():
                def send_halo(t, carry):
                    for a in (1, 2):
                        halo_in(a, t // group, lax.rem(t, group), me - (group - HOPS)).start()
                    return carry

                lax.fori_loop(0, heads_here * group, send_halo, 0)

        pos = lax.broadcasted_iota(jnp.int32, (rows, 1), 0)

        def zeros_in(which):
            ids = seg[pl.ds(which, 1), :]
            return jnp.sum(jnp.where(ids == 0, 1.0, 0.0), axis=1, keepdims=True).astype(jnp.int32)

        def low_of(b, cut):
            first = (base + b) * rows
            return jnp.where(pos + first >= cut, cut, 0) - first

        def z_copy(h, b, slot):
            return pltpu.make_async_remote_copy(
                src_ref=fb.at[h, rows_of(b)],
                dst_ref=xb.at[h, rows_of(b)],
                send_sem=z_send.at[h, slot],
                recv_sem=z_recv.at[h, slot],
                device_id=(c, ahead),
                device_id_type=MESH,
            )

        own_cut = zeros_in(s)
        start = lax.rem(me + group - HOPS, group)

        def layer_one(t, h):
            i = 2 * t

            @pl.when(i == 0)
            def _():
                for a in range(3):
                    own_copy(a, h).wait()

                def arrived(k, inner):
                    for a in range(3):
                        in_copy(a, h, k, lax.rem(me + group - k, group)).wait_recv()
                    return inner

                lax.fori_loop(1, group, arrived, 0)
                if groups > 1:
                    for a in (1, 2):
                        for j in range(HOPS):
                            halo_in(a, h, j, j).wait_recv()

            tiles = [lax.rem(start + i + j, group) for j in range(2)]
            results = attend_all(
                [
                    (
                        qb[h, rows_of(b)],
                        kb[h, rows_of(b, HOPS + 1)],
                        vb[h, rows_of(b, HOPS + 1)],
                        low_of(b, own_cut),
                    )
                    for b in tiles
                ],
                1.0 / math.sqrt(HD),
                True,
            )
            for j, (b, result) in enumerate(zip(tiles, results)):
                fb[h, rows_of(b)] = result
                z_copy(h, b, i + j).start()
                if groups > 1:
                    @pl.when(b >= group - HOPS)
                    def _():
                        halo_z(h, b - (group - HOPS), b).start()
            return h

        prior_cut = zeros_in(behind)

        def normalize(x):
            x = x.astype(jnp.float32)
            mean = jnp.mean(x * x, axis=1, keepdims=True)
            return (x * lax.rsqrt(mean + 1e-06)).astype(jnp.bfloat16)

        def gained(normed, gain, h):
            g = gain[:, cols_of(me, h)].astype(jnp.float32)
            return (normed.astype(jnp.float32) * g).astype(jnp.bfloat16)

        def take(h, slot):
            b = lax.rem(start + slot, group)
            z_copy(h, b, slot).wait_recv()
            normed = normalize(xb[h, rows_of(b)])
            nb[h, rows_of(b + HOPS)] = normed
            k2b[h, rows_of(b + HOPS)] = gained(normed, gk, h)

        def out_copy(h, k):
            return pltpu.make_async_remote_copy(
                src_ref=ob.at[h, rows_of(lax.rem(me + k, group))],
                dst_ref=out.at[0, :, cols_of(me, h)],
                send_sem=o_send.at[h, k],
                recv_sem=o_recv.at[h, k],
                device_id=(peer(k), s),
                device_id_type=MESH,
            )

        def out_own(h):
            return pltpu.make_async_copy(
                ob.at[h, rows_of(me)], out.at[0, :, cols_of(me, h)], o_recv.at[h, 0]
            )

        def layer_two(t, h):
            i = 2 * t

            @pl.when(i == 0)
            def _():
                if groups > 1:
                    for j in range(HOPS):
                        halo_z(h, j, j).wait_recv()
                        normed = normalize(nb[h, rows_of(j)])
                        nb[h, rows_of(j)] = normed
                        k2b[h, rows_of(j)] = gained(normed, gk, h)

                def first_ones(slot, inner):
                    take(h, slot)
                    return inner

                lax.fori_loop(0, HOPS, first_ones, 0)

            for j in range(2):
                @pl.when(i + j < group - HOPS)
                def _():
                    take(h, i + j + HOPS)

            tiles = [lax.rem(me + i + j, group) for j in range(2)]
            normed = [nb[h, rows_of(b + HOPS)] for b in tiles]
            results = attend_all(
                [
                    (
                        gained(own, gq, h),
                        k2b[h, rows_of(b, HOPS + 1)],
                        nb[h, rows_of(b, HOPS + 1)],
                        low_of(b, prior_cut),
                    )
                    for b, own in zip(tiles, normed)
                ],
                1.0 / HD,
                False,
            )
            for b, own, second in zip(tiles, normed, results):
                mixed = second.astype(jnp.float32) + own.astype(jnp.float32)
                ob[h, rows_of(b)] = mixed.astype(jnp.bfloat16)

            @pl.when(i == 0)
            def _():
                out_own(h).start()

            @pl.when(i > 0)
            def _():
                out_copy(h, i).start()

            out_copy(h, i + 1).start()
            return h

        def both_layers(h, carry):
            lax.fori_loop(0, half, layer_one, h)
            lax.fori_loop(0, half, layer_two, h)
            return carry

        lax.fori_loop(0, heads_here, both_layers, 0)

        def finish(t, carry):
            h = t // (group - 1)
            k = 1 + lax.rem(t, group - 1)
            for a in range(3):
                in_copy(a, h, k, me).wait_send()
            out_copy(h, k).wait_send()
            p = lax.rem(me + group - k, group)
            pltpu.make_async_remote_copy(
                src_ref=ob.at[h, rows_of(me)],
                dst_ref=out.at[0, :, cols_of(p, h)],
                send_sem=o_send.at[h, k],
                recv_sem=o_recv.at[h, k],
                device_id=(peer(k), s),
                device_id_type=MESH,
            ).wait_recv()
            return carry

        lax.fori_loop(0, heads_here * (group - 1), finish, 0)

        def finish_z(t, carry):
            h = t // group
            i = lax.rem(t, group)
            z_copy(h, lax.rem(start + i, group), i).wait_send()
            return carry

        lax.fori_loop(0, heads_here * group, finish_z, 0)
        for h in range(heads_here):
            out_own(h).wait()
            if groups > 1:
                for j in range(HOPS):
                    halo_z(h, j, group - HOPS + j).wait_send()
        if groups > 1:
            @pl.when(me >= group - HOPS)
            def _():
                def sent_halo(t, carry):
                    for a in (1, 2):
                        halo_in(a, t // group, lax.rem(t, group), me - (group - HOPS)).wait_send()
                    return carry

                lax.fori_loop(0, heads_here * group, sent_halo, 0)

    return kernel


def solution(mesh):
    ctx = mesh.shape["ctx"]
    sections = mesh.shape["section"]
    group = math.gcd(ctx, 8)

    def per_device(queries, keys, values, segments, gain_query, gain_key):
        _, rows, width = queries.shape
        heads_here = width // HD // group
        padded = (group + HOPS) * rows
        bf = jnp.bfloat16
        dma = pltpu.SemaphoreType.DMA
        scratch = [
            pltpu.VMEM((heads_here, group * rows, HD), bf),
            pltpu.VMEM((heads_here, padded, HD), bf),
            pltpu.VMEM((heads_here, padded, HD), bf),
            pltpu.VMEM((heads_here, group * rows, HD), bf),
            pltpu.VMEM((heads_here, group * rows, HD), bf),
            pltpu.VMEM((heads_here, padded, HD), bf),
            pltpu.VMEM((heads_here, padded, HD), bf),
            pltpu.VMEM((heads_here, group * rows, HD), bf),
            pltpu.VMEM(segments.shape, segments.dtype),
            pltpu.VMEM(gain_query.shape, bf),
            pltpu.VMEM(gain_key.shape, bf),
            dma((3,)),
            dma((3, heads_here, group)),
            dma((3, heads_here, group)),
            dma((heads_here, group)),
            dma((heads_here, group)),
            dma((heads_here, group)),
            dma((heads_here, group)),
        ]
        if ctx > group:
            scratch += [
                dma((2, heads_here, group)),
                dma((2, heads_here, HOPS)),
                dma((heads_here, HOPS)),
                dma((heads_here, HOPS)),
            ]
        return pl.pallas_call(
            make_kernel(ctx, sections, group, rows, heads_here),
            out_shape=jax.ShapeDtypeStruct(queries.shape, bf),
            in_specs=[pl.BlockSpec(memory_space=pltpu.HBM)] * 6,
            out_specs=pl.BlockSpec(memory_space=pl.ANY),
            scratch_shapes=scratch,
            compiler_params=pltpu.CompilerParams(
                collective_id=0, has_side_effects=True, vmem_limit_bytes=60 * 1024 * 1024
            ),
        )(queries, keys, values, segments, gain_query, gain_key)

    return jax.shard_map(
        per_device,
        mesh=mesh,
        in_specs=(
            P("section", "ctx", None),
            P("section", "ctx", None),
            P("section", "ctx", None),
            P(),
            P("section", None),
            P("section", None),
        ),
        out_specs=P("section", "ctx", None),
        check_vma=False,
    )
```
